256 devices in a mesh: space: 32 (over z_hi, x, core), mode: 8 (over z_lo, y).
Axes of the slice: x: 4, y: 4, z: 8 (z_hi: 4, z_lo: 2; z = z_hi * 2 + z_lo), core: 2. Of those that a mesh axis runs over, the one named last changes fastest.
Arguments:
- field: float32 [3, 16, 256, 64, 256], P(None, 'mode', 'space'), may hold values from -6 to 6
- velocity: float32 [256, 64, 256], P('space'), may hold values from 0.1 to 1
- dispersion: float32 [256, 64, 256], P('space'), may hold values from 0.05 to 0.3
- mobility: float32 [3, 8, 16], replicated, may hold values from -0.2 to 0.2
- material: int32 [256, 64, 256], P('space'), may hold values from 0 to 7
- fixed_mask: int32 [256, 64, 256], P('space'), may hold values 0 or 1
Outputs:
- advanced: float32 [3, 16, 256, 64, 256], P(None, 'mode', 'space')
The draws below stay inside these ranges and needn't reach their ends.
All inputs are finite; a program needn't handle non-finite values. No bound on the sum of `fixed_mask` on one device may be relied on, other than what follows from the above.
Results may differ from the reference program's by a relative error of at most 0.0001.
Values sent between devices are 32-bit elements; how exact they have to be, the bound alone decides.
No kernel may reach another device: no remote copies, remote signals or barrier semaphores. Data moves between devices by JAX's collectives and lax.ppermute only.
A program may use at most 64 MiB of HBM per device.

```python
import math
import jax
import jax.numpy as jnp
from jax import lax

METALS = 3
MODES = 16
CLASSES = 8
NY = 64
NZ = 256
STEPS = 2
NX = 256


def place_ends(values, own_key, smallest, top_value):
    index_at = [jax.random.randint(jax.random.fold_in(own_key, axis), (), 0, length) for axis, length in enumerate(values.shape)]
    longest = values.shape.index(max(values.shape))
    beside = index_at[:longest] + [(index_at[longest] + 1) % values.shape[longest]] + index_at[longest + 1:]
    return values.at[tuple(index_at)].set(smallest).at[tuple(beside)].set(top_value)


def shard_levels(stream_key, shape, split, smallest, high):
    factor_of, own = 1.0, jax.random.fold_in(stream_key, 6)
    for position, blocks in split:
        steps = jnp.exp(jax.random.uniform(jax.random.fold_in(own, position), (blocks,), jnp.float32, smallest / len(split), high / len(split)))
        factor_of = factor_of * jnp.repeat(steps, shape[position] // blocks).reshape([-1 if axis == position else 1 for axis in range(len(shape))])
    return factor_of


def centred(own_key, extent, scale, limit, pieces=(), held_as=jnp.bfloat16):
    values = scale * jax.random.normal(own_key, extent, jnp.float32)
    if pieces:
        values = values * shard_levels(own_key, extent, pieces, -0.22, 0.18)
    return jnp.clip(values, -limit, limit).astype(held_as)


def setup_inputs(seed: int = 0) -> dict:
    splits = jax.random.split(jax.random.key(seed), 7)
    return {
        "field": centred(splits[0], (METALS, MODES, NX, NY, NZ), 1.0, 6.0, ((1, 8), (2, 32)), jnp.float32),
        "velocity": jnp.clip(jnp.exp(math.log(1.0) - 2.3025851 * jax.random.uniform(splits[1], (NX, NY, NZ), jnp.float32) ** shard_levels(splits[1], (NX, NY, NZ), ((0, 32),), -0.2, 0.2)), 0.1, 1.0),
        "dispersion": jnp.clip(jnp.exp(math.log(0.3) - 1.7917595 * jax.random.uniform(splits[2], (NX, NY, NZ), jnp.float32) ** shard_levels(splits[2], (NX, NY, NZ), ((0, 32),), -0.2, 0.2)), 0.05, 0.3),
        "mobility": jnp.clip(jax.random.uniform(splits[3], (METALS, CLASSES, MODES), jnp.float32, -0.2, 0.2), -0.2, 0.2),
        "material": place_ends(jax.random.randint(splits[4], (NX, NY, NZ), 0, CLASSES), jax.random.fold_in(splits[4], 1), 0, CLASSES - 1).astype(jnp.int32),
        "fixed_mask": place_ends((jax.random.randint(splits[5], (NX, NY, NZ), 0, 8) < 1).astype(jnp.int32), jax.random.fold_in(splits[5], 1), 0, 1),
    }


TIME_STEP = 0.1
MOBILE_BASE = 0.7

def legendre_weight(order):
    return math.comb(2 * order, order) / 4.0 ** order

def triple_table(terms_count):
    entries = []
    for degree_a in range(terms_count):
        slab_values = []
        for degree_b in range(terms_count):
            row_values = []
            for degree_c in range(terms_count):
                degree_sum = degree_a + degree_b + degree_c
                halfsum = degree_sum // 2
                amount = 0.0
                if degree_sum % 2 == 0 and halfsum >= degree_a and (halfsum >= degree_b) and (halfsum >= degree_c):
                    amount = legendre_weight(halfsum - degree_a) * legendre_weight(halfsum - degree_b) * legendre_weight(halfsum - degree_c)
                    amount = amount / legendre_weight(halfsum) / (degree_sum + 1)
                    amount = amount * math.sqrt((2 * degree_a + 1) * (2 * degree_b + 1) * (2 * degree_c + 1))
                row_values.append(amount)
            slab_values.append(row_values)
        entries.append(slab_values)
    return jnp.asarray(entries, jnp.float32)

def operate(values, velocity, dispersion):
    padded = jnp.pad(values, ((0, 0), (2, 2), (1, 1), (1, 1)))
    middle = padded[:, 2:-2, 1:-1, 1:-1]
    left_two = padded[:, :-4, 1:-1, 1:-1]
    left_one = padded[:, 1:-3, 1:-1, 1:-1]
    right_one = padded[:, 3:-1, 1:-1, 1:-1]
    right_two = padded[:, 4:, 1:-1, 1:-1]
    lower_y = padded[:, 2:-2, :-2, 1:-1]
    upper_y = padded[:, 2:-2, 2:, 1:-1]
    lower_z = padded[:, 2:-2, 1:-1, :-2]
    upper_z = padded[:, 2:-2, 1:-1, 2:]
    spread = (16.0 * (left_one + right_one) - (left_two + right_two) - 30.0 * middle) / 12.0
    spread = spread + (lower_y + upper_y) + (lower_z + upper_z) - 4.0 * middle
    carried = (2.0 * right_one + 3.0 * middle - 6.0 * left_one + left_two) / 6.0
    return dispersion * spread - velocity * carried

def reference(field, velocity, dispersion, mobility, material, fixed_mask):
    modes = mobility.shape[2]
    triple = triple_table(modes)
    movable = (1 - fixed_mask).astype(jnp.float32)
    state = field
    for sweep_index in range(STEPS):
        updated = []
        for metal in range(METALS):
            operated = operate(state[metal], velocity, dispersion)
            coeffs = jnp.moveaxis(mobility[metal][material], -1, 0)
            flat = operated.reshape(modes, -1)
            coupled = MOBILE_BASE * flat
            for term in range(modes):
                mixed = jnp.dot(triple[:, :, term], flat, precision=lax.Precision.HIGHEST)
                coupled = coupled + coeffs[term].reshape(1, -1) * mixed
            updated.append(state[metal] + TIME_STEP * movable * coupled.reshape(operated.shape))
        state = jnp.stack(updated)
    return state
```

```python
import functools
import math

import jax
import jax.numpy as jnp
import numpy as np
from jax import lax
from jax.experimental import pallas as pl
from jax.experimental.pallas import tpu as pltpu
from jax.sharding import PartitionSpec as P


TIME_STEP = 0.1
MOBILE_BASE = 0.7
CHUNKS = ((0, 1), (1, 1), (2, 1))
VMEM_LIMIT = 40 * 1024 * 1024


def legendre_weight(order):
    return math.comb(2 * order, order) / 4.0**order


def triple_table(terms_count):
    table = np.zeros((terms_count,) * 3, np.float64)
    for a in range(terms_count):
        for b in range(terms_count):
            for c in range(terms_count):
                total = a + b + c
                half = total // 2
                if total % 2 == 0 and max(a, b, c) <= half:
                    amount = legendre_weight(half - a) * legendre_weight(half - b) * legendre_weight(half - c)
                    amount = amount / legendre_weight(half) / (total + 1)
                    table[a, b, c] = amount * math.sqrt((2 * a + 1) * (2 * b + 1) * (2 * c + 1))
    return table.astype(np.float32)


def class_weights(mobility):
    metals, classes, modes = mobility.shape
    triple = jnp.asarray(triple_table(modes))
    mats = jnp.einsum("ijk,mck->mcij", triple, mobility, precision=lax.Precision.HIGHEST)
    mats = TIME_STEP * (mats + MOBILE_BASE * jnp.eye(modes, dtype=jnp.float32))
    mats = mats.reshape(metals, classes * modes, modes)
    high = lax.reduce_precision(mats, exponent_bits=8, mantissa_bits=7)
    return jnp.concatenate([high, high, mats - high], axis=2).astype(jnp.bfloat16)


def lane_neighbours(v):
    lane = lax.broadcasted_iota(jnp.int32, v.shape, v.ndim - 1)
    size = v.shape[-1]
    lower = jnp.where(lane == 0, 0.0, pltpu.roll(v, 1, v.ndim - 1))
    upper = jnp.where(lane == size - 1, 0.0, pltpu.roll(v, size - 1, v.ndim - 1))
    return lower + upper


def combine(l2, l1, mid, r1, r2, sides, vel, disp):
    spread = (16.0 / 12.0) * (l1 + r1) - (1.0 / 12.0) * (l2 + r2) - 6.5 * mid + sides
    carried = (1.0 / 3.0) * r1 + 0.5 * mid - l1 + (1.0 / 6.0) * l2
    return disp * spread - vel * carried


def spread_kernel(f_ref, lo_ref, hi_ref, vel_ref, disp_ref, out_ref):
    depth, rows, width = f_ref.shape[2:]
    blocks = out_ref.shape[0]
    part = rows // blocks
    row = lax.broadcasted_iota(jnp.int32, (rows, width), 0)

    def layer(x):
        if x < 0:
            return lo_ref[0, 0, x + 2]
        if x >= depth:
            return hi_ref[0, 0, x - depth]
        return f_ref[0, 0, x]

    zero_row = jnp.zeros((1, width), jnp.float32)
    for x in range(depth):
        mid = layer(x)
        sides = lane_neighbours(mid)
        sides += jnp.where(row == 0, 0.0, pltpu.roll(mid, 1, 0))
        sides += jnp.where(row == rows - 1, 0.0, pltpu.roll(mid, rows - 1, 0))
        value = combine(
            layer(x - 2), layer(x - 1), mid, layer(x + 1), layer(x + 2), sides, vel_ref[x], disp_ref[x]
        )
        for b in range(blocks):
            out_ref[b, 0, 0, x] = value[b * part : (b + 1) * part]
            below = value[b * part - 1 : b * part] if b else zero_row
            above = value[(b + 1) * part : (b + 1) * part + 1] if b < blocks - 1 else zero_row
            out_ref[b, 0, 0, depth, x : x + 1] = below
            out_ref[b, 0, 0, depth + 1, x : x + 1] = above


def couple(value, weights, classes, cls_row):
    modes, width = value.shape
    high = value.astype(jnp.bfloat16)
    low = (value - high.astype(jnp.float32)).astype(jnp.bfloat16)
    stacked = jnp.concatenate([high, low, high], axis=0)
    mixed = jnp.dot(weights, stacked, preferred_element_type=jnp.float32)
    picked = jnp.broadcast_to(cls_row, (modes, width))
    total = jnp.zeros((modes, width), jnp.float32)
    for c in range(classes):
        total = jnp.where(picked == c, mixed[c * modes : (c + 1) * modes], total)
    return total


def first_kernel(r_ref, w_ref, cls_ref, g_ref, l_ref, lo_ref, hi_ref):
    sources, _, each, slots, part, width = r_ref.shape
    modes = sources * each
    depth = slots - 2
    classes = w_ref.shape[1] // modes
    weights = w_ref[0]
    for s in range(slots):
        values = jnp.swapaxes(r_ref[:, 0, :, s].reshape(modes, part, width), 0, 1)
        for y in range(part):
            got = couple(values[y], weights, classes, cls_ref[s, y : y + 1])
            if s < depth:
                l_ref[0, s, y] = values[y]
                g_ref[0, s, y + 1] = got
                if s < 2:
                    lo_ref[0, s, y] = got
                if s >= depth - 2:
                    hi_ref[0, s - depth + 2, y] = got
            elif s == depth:
                g_ref[0, y, 0] = got
            else:
                g_ref[0, y, part + 1] = got


def second_kernel(g_ref, l_ref, lo_ref, hi_ref, w_ref, cls_ref, vel_ref, disp_ref, out_ref):
    _, depth, padded_rows, modes, width = g_ref.shape
    part = padded_rows - 2
    targets, _, each = out_ref.shape[:3]
    classes = w_ref.shape[1] // modes
    weights = w_ref[0]

    def at(x, y):
        if x < 0:
            return lo_ref[0, x + 2, y]
        if x >= depth:
            return hi_ref[0, x - depth, y]
        return g_ref[0, x, y + 1]

    for x in range(depth):
        rows = []
        for y in range(part):
            mid = at(x, y)
            sides = lane_neighbours(mid) + (g_ref[0, x, y] + g_ref[0, x, y + 2])
            vel = jnp.broadcast_to(vel_ref[x, y : y + 1], (modes, width))
            disp = jnp.broadcast_to(disp_ref[x, y : y + 1], (modes, width))
            value = combine(at(x - 2, y), at(x - 1, y), mid, at(x + 1, y), at(x + 2, y), sides, vel, disp)
            value += 2.0 * l_ref[0, x, y]
            rows.append(couple(value, weights, classes, cls_ref[x, y : y + 1]))
        out_ref[:, 0, :, x] = jnp.swapaxes(jnp.stack(rows), 0, 1).reshape(targets, each, part, width)


def last_kernel(f_ref, r_ref, *rest):
    out_ref = rest[-1]
    blocks = r_ref.shape[0]
    part = r_ref.shape[4]
    for b in range(blocks):
        rows = slice(b * part, (b + 1) * part)
        out_ref[0, 0, :, rows] = f_ref[0, 0, :, rows] + r_ref[b, 0, 0]


def whole(array):
    return pl.BlockSpec(array.shape, lambda *_: (0,) * array.ndim)


def params(grid):
    return pltpu.CompilerParams(dimension_semantics=("arbitrary",) * grid, vmem_limit_bytes=VMEM_LIMIT)


def cost(flops, *arrays):
    moved = sum(math.prod(a.shape) * 4 for a in arrays)
    return pl.CostEstimate(flops=flops, bytes_accessed=moved, transcendentals=0)


def on_device(field, velocity, dispersion, mobility, material, fixed_mask):
    metals, each, depth, rows, width = field.shape
    modes = mobility.shape[2]
    classes = mobility.shape[1]
    blocks = lax.axis_size("mode")
    part = rows // blocks
    space = lax.axis_size("space")
    up = [(i, i + 1) for i in range(space - 1)]
    down = [(i + 1, i) for i in range(space - 1)]

    weights = class_weights(mobility)
    here = lax.axis_index("mode") * part
    cls = jnp.where(fixed_mask == 1, classes, material)
    cls = jnp.pad(cls, ((0, 0), (1, 1), (0, 0)))
    cls = lax.dynamic_slice_in_dim(cls, here, part + 2, 1)
    cls = jnp.concatenate([cls[:, 1:-1], cls[None, :, 0], cls[None, :, -1]], axis=0)
    vel = lax.dynamic_slice_in_dim(velocity, here, part, 1)
    disp = lax.dynamic_slice_in_dim(dispersion, here, part, 1)

    def row_block(shape, count=None):
        return pl.BlockSpec(shape, lambda m: (m,) + (0,) * (len(shape) - 1))

    halos = []
    for first, count in CHUNKS:
        some = field[first : first + count]
        halos.append(
            (
                lax.ppermute(some[:, :, depth - 2 :], "space", up),
                lax.ppermute(some[:, :, :2], "space", down),
            )
        )

    arrived = []
    for (first, count), (lo, hi) in zip(CHUNKS, halos):
        sent = jax.ShapeDtypeStruct((blocks, count, each, depth + 2, part, width), jnp.float32)
        spread = pl.pallas_call(
            spread_kernel,
            grid=(count, each),
            in_specs=[
                pl.BlockSpec((1, 1, depth, rows, width), lambda m, e, first=first: (m + first, e, 0, 0, 0)),
                pl.BlockSpec((1, 1, 2, rows, width), lambda m, e: (m, e, 0, 0, 0)),
                pl.BlockSpec((1, 1, 2, rows, width), lambda m, e: (m, e, 0, 0, 0)),
                whole(velocity),
                whole(dispersion),
            ],
            out_specs=pl.BlockSpec((blocks, 1, 1, depth + 2, part, width), lambda m, e: (0, m, e, 0, 0, 0)),
            out_shape=sent,
            compiler_params=params(2),
            cost_estimate=cost(20 * math.prod(sent.shape), sent, sent),
            name="spread",
        )(field, lo, hi, velocity, dispersion)
        arrived.append(lax.all_to_all(spread, "mode", split_axis=0, concat_axis=0, tiled=True))

    mixed = []
    for (first, count), got in zip(CHUNKS, arrived):
        shapes = [
            jax.ShapeDtypeStruct((count, depth, part + 2, modes, width), jnp.float32),
            jax.ShapeDtypeStruct((count, depth, part, modes, width), jnp.float32),
            jax.ShapeDtypeStruct((count, 2, part, modes, width), jnp.float32),
            jax.ShapeDtypeStruct((count, 2, part, modes, width), jnp.float32),
        ]
        g, l, low_side, high_side = pl.pallas_call(
            first_kernel,
            grid=(count,),
            in_specs=[
                pl.BlockSpec((blocks, 1) + got.shape[2:], lambda m: (0, m, 0, 0, 0, 0)),
                pl.BlockSpec((1,) + weights.shape[1:], lambda m, first=first: (m + first, 0, 0)),
                whole(cls),
            ],
            out_specs=[row_block((1,) + s.shape[1:]) for s in shapes],
            out_shape=shapes,
            compiler_params=params(1),
            cost_estimate=cost(300 * math.prod(got.shape), got, *shapes),
            name="first",
        )(got, weights, cls)
        lo = lax.ppermute(high_side, "space", up)
        hi = lax.ppermute(low_side, "space", down)
        mixed.append((g, l, lo, hi))

    back = []
    for (first, count), (g, l, lo, hi) in zip(CHUNKS, mixed):
        sent = jax.ShapeDtypeStruct((blocks, count, each, depth, part, width), jnp.float32)
        second = pl.pallas_call(
            second_kernel,
            grid=(count,),
            in_specs=[row_block((1,) + a.shape[1:]) for a in (g, l, lo, hi)]
            + [
                pl.BlockSpec((1,) + weights.shape[1:], lambda m, first=first: (m + first, 0, 0)),
                whole(cls),
                whole(vel),
                whole(disp),
            ],
            out_specs=pl.BlockSpec((blocks, 1) + sent.shape[2:], lambda m: (0, m, 0, 0, 0, 0)),
            out_shape=sent,
            compiler_params=params(1),
            cost_estimate=cost(300 * math.prod(sent.shape), g, l, sent),
            name="second",
        )(g, l, lo, hi, weights, cls, vel, disp)
        back.append(lax.all_to_all(second, "mode", split_axis=0, concat_axis=0, tiled=True))

    out = None
    for (first, count), got in zip(CHUNKS, back):
        block = pl.BlockSpec((1, 1, depth, rows, width), lambda m, e, first=first: (m + first, e, 0, 0, 0))
        operands = [field, got]
        specs = [block, pl.BlockSpec((blocks, 1, 1, depth, part, width), lambda m, e: (0, m, e, 0, 0, 0))]
        aliases = {}
        if out is not None:
            operands.append(out)
            specs.append(pl.BlockSpec(memory_space=pl.ANY))
            aliases = {2: 0}
        out = pl.pallas_call(
            last_kernel,
            grid=(count, each),
            in_specs=specs,
            out_specs=block,
            out_shape=jax.ShapeDtypeStruct(field.shape, jnp.float32),
            input_output_aliases=aliases,
            compiler_params=params(2),
            cost_estimate=cost(math.prod(got.shape), got, got, got),
            name="last",
        )(*operands)
    return out


def solution(mesh):
    in_specs = (
        P(None, "mode", "space", None, None),
        P("space", None, None),
        P("space", None, None),
        P(),
        P("space", None, None),
        P("space", None, None),
    )
    out_specs = P(None, "mode", "space", None, None)
    return jax.shard_map(
        on_device, mesh=mesh, in_specs=in_specs, out_specs=out_specs, check_vma=False
    )
```

```python
import functools
import math

import jax
import jax.numpy as jnp
import numpy as np
from jax import lax
from jax.experimental import pallas as pl
from jax.experimental.pallas import tpu as pltpu
from jax.sharding import PartitionSpec as P


TIME_STEP = 0.1
MOBILE_BASE = 0.7
VMEM_LIMIT = 30 * 1024 * 1024


def legendre_weight(order):
    return math.comb(2 * order, order) / 4.0**order


def triple_table(terms_count):
    table = np.zeros((terms_count,) * 3, np.float64)
    for a in range(terms_count):
        for b in range(terms_count):
            for c in range(terms_count):
                total = a + b + c
                half = total // 2
                if total % 2 == 0 and max(a, b, c) <= half:
                    amount = legendre_weight(half - a) * legendre_weight(half - b) * legendre_weight(half - c)
                    amount = amount / legendre_weight(half) / (total + 1)
                    table[a, b, c] = amount * math.sqrt((2 * a + 1) * (2 * b + 1) * (2 * c + 1))
    return table.astype(np.float32)


def class_weights(mobility):
    metals, classes, modes = mobility.shape
    triple = jnp.asarray(triple_table(modes))
    mats = jnp.einsum("ijk,mck->mcij", triple, mobility, precision=lax.Precision.HIGHEST)
    mats = TIME_STEP * (mats + MOBILE_BASE * jnp.eye(modes, dtype=jnp.float32))
    mats = mats.reshape(metals, classes * modes, modes)
    high = lax.reduce_precision(mats, exponent_bits=8, mantissa_bits=7)
    return jnp.concatenate([high, high, mats - high], axis=2).astype(jnp.bfloat16)


def lane_neighbours(v):
    lane = lax.broadcasted_iota(jnp.int32, v.shape, v.ndim - 1)
    size = v.shape[-1]
    lower = jnp.where(lane == 0, 0.0, pltpu.roll(v, 1, v.ndim - 1))
    upper = jnp.where(lane == size - 1, 0.0, pltpu.roll(v, size - 1, v.ndim - 1))
    return lower + upper


def combine(l2, l1, mid, r1, r2, sides, vel, disp):
    spread = (16.0 / 12.0) * (l1 + r1) - (1.0 / 12.0) * (l2 + r2) - 6.5 * mid + sides
    carried = (1.0 / 3.0) * r1 + 0.5 * mid - l1 + (1.0 / 6.0) * l2
    return disp * spread - vel * carried


def spread_kernel(layers, f_ref, vel_ref, disp_ref, *rest):
    lo_ref, hi_ref = rest[:2] if len(rest) == 3 else (None, None)
    out_ref = rest[-1]
    depth, rows, width = f_ref.shape[2:]
    blocks = out_ref.shape[0]
    part = rows // blocks
    count = len(layers)
    row = lax.broadcasted_iota(jnp.int32, (rows, width), 0)

    def layer(e, x):
        if x < 0:
            return lo_ref[0, e, x + 2]
        if x >= depth:
            return hi_ref[0, e, x - depth]
        return f_ref[0, e, x]

    zero_row = jnp.zeros((1, width), jnp.float32)
    for e in range(f_ref.shape[1]):
        for i, x in enumerate(layers):
            mid = layer(e, x)
            sides = lane_neighbours(mid)
            sides += jnp.where(row == 0, 0.0, pltpu.roll(mid, 1, 0))
            sides += jnp.where(row == rows - 1, 0.0, pltpu.roll(mid, rows - 1, 0))
            around = [layer(e, x + k) for k in (-2, -1, 0, 1, 2)]
            value = combine(*around, sides, vel_ref[x], disp_ref[x])
            for b in range(blocks):
                out_ref[b, 0, e, i] = value[b * part : (b + 1) * part]
                below = value[b * part - 1 : b * part] if b else zero_row
                above = value[(b + 1) * part : (b + 1) * part + 1] if b < blocks - 1 else zero_row
                out_ref[b, 0, e, count, i : i + 1] = below
                out_ref[b, 0, e, count, count + i : count + i + 1] = above


def couple(value, weights, classes, cls_row):
    modes, width = value.shape
    high = value.astype(jnp.bfloat16)
    low = (value - high.astype(jnp.float32)).astype(jnp.bfloat16)
    stacked = jnp.concatenate([high, low, high], axis=0)
    mixed = jnp.dot(weights, stacked, preferred_element_type=jnp.float32)
    picked = jnp.broadcast_to(cls_row, (modes, width))
    total = jnp.zeros((modes, width), jnp.float32)
    for c in range(classes):
        total = jnp.where(picked == c, mixed[c * modes : (c + 1) * modes], total)
    return total


def first_kernel(layers, r_ref, w_ref, cls_ref, l_ref, beside_ref, *g_refs):
    sources, _, each, slots, part, width = r_ref.shape
    modes = sources * each
    count = len(layers)
    share = count // len(g_refs)
    classes = w_ref.shape[1] // modes
    weights = w_ref[0]
    for s in range(slots):
        values = jnp.swapaxes(r_ref[:, 0, :, s].reshape(modes, part, width), 0, 1)
        for y in range(part):
            if s < count:
                x, row = layers[s], y + 1
            else:
                x, row = layers[y % count], (part + 1) * (y // count)
            got = couple(values[y], weights, classes, cls_ref[x, row : row + 1])
            if s < count:
                l_ref[0, s, y] = values[y]
                g_refs[s // share][0, s % share, y] = got
            else:
                beside_ref[0, y % count, y // count] = got


def second_kernel(layers, g_ref, low_ref, high_ref, l_ref, beside_ref, w_ref, cls_ref, vel_ref, disp_ref, *rest):
    lo_ref, hi_ref = rest[:2] if len(rest) == 3 else (None, None)
    out_ref = rest[-1]
    inner, part, modes, width = g_ref.shape[1:]
    depth = inner + 4
    targets, _, each = out_ref.shape[:3]
    classes = w_ref.shape[1] // modes
    weights = w_ref[0]

    def at(x, y):
        if x < 0:
            return lo_ref[0, x + 2, y]
        if x < 2:
            return low_ref[0, x, y]
        if x < depth - 2:
            return g_ref[0, x - 2, y]
        if x < depth:
            return high_ref[0, x - depth + 2, y]
        return hi_ref[0, x - depth, y]

    for i, x in enumerate(layers):
        rows = []
        for y in range(part):
            mid = at(x, y)
            below = at(x, y - 1) if y else beside_ref[0, i, 0]
            above = at(x, y + 1) if y < part - 1 else beside_ref[0, i, 1]
            sides = lane_neighbours(mid) + (below + above)
            vel = jnp.broadcast_to(vel_ref[x, y : y + 1], (modes, width))
            disp = jnp.broadcast_to(disp_ref[x, y : y + 1], (modes, width))
            value = combine(at(x - 2, y), at(x - 1, y), mid, at(x + 1, y), at(x + 2, y), sides, vel, disp)
            value += 2.0 * l_ref[0, i, y]
            rows.append(couple(value, weights, classes, cls_ref[x, y + 1 : y + 2]))
        out_ref[:, 0, :, i] = jnp.swapaxes(jnp.stack(rows), 0, 1).reshape(targets, each, part, width)


def last_kernel(f_ref, r_ref, *rest):
    out_ref = rest[-1]
    blocks = r_ref.shape[0]
    part = r_ref.shape[4]
    for b in range(blocks):
        rows = slice(b * part, (b + 1) * part)
        out_ref[0, :, :, rows] = f_ref[0, :, :, rows] + r_ref[b, 0]


def whole(array):
    return pl.BlockSpec(array.shape, lambda *_: (0,) * array.ndim)


def params(grid):
    return pltpu.CompilerParams(dimension_semantics=("arbitrary",) * grid, vmem_limit_bytes=VMEM_LIMIT)


def cost(flops, *arrays):
    moved = sum(math.prod(a.shape) * 4 for a in arrays)
    return pl.CostEstimate(flops=flops, bytes_accessed=moved, transcendentals=0)


def on_device(field, velocity, dispersion, mobility, material, fixed_mask):
    metals, each, depth, rows, width = field.shape
    modes = mobility.shape[2]
    classes = mobility.shape[1]
    blocks = lax.axis_size("mode")
    part = rows // blocks
    space = lax.axis_size("space")
    up = [(i, i + 1) for i in range(space - 1)]
    down = [(i + 1, i) for i in range(space - 1)]
    inner = tuple(range(2, depth - 2))
    outer = (0, 1, depth - 2, depth - 1)
    after = lax.optimization_barrier

    weights = class_weights(mobility)
    here = lax.axis_index("mode") * part
    cls = jnp.where(fixed_mask == 1, classes, material)
    cls = lax.dynamic_slice_in_dim(jnp.pad(cls, ((0, 0), (1, 1), (0, 0))), here, part + 2, 1)
    vel = lax.dynamic_slice_in_dim(velocity, here, part, 1)
    disp = lax.dynamic_slice_in_dim(dispersion, here, part, 1)

    def f32(*shape):
        return jax.ShapeDtypeStruct(shape, jnp.float32)

    def by_metal(array):
        return pl.BlockSpec((1,) + array.shape[1:], lambda m: (m,) + (0,) * (len(array.shape) - 1))

    def over_modes(array):
        return lax.all_to_all(array, "mode", split_axis=0, concat_axis=0, tiled=True)

    def run_spread(layers, *halos):
        sent = f32(blocks, metals, each, len(layers) + 1, part, width)
        operands = (field, velocity, dispersion) + halos
        return pl.pallas_call(
            functools.partial(spread_kernel, layers),
            grid=(metals,),
            in_specs=[by_metal(field), whole(velocity), whole(dispersion)] + [by_metal(h) for h in halos],
            out_specs=pl.BlockSpec((blocks, 1) + sent.shape[2:], lambda m: (0, m, 0, 0, 0, 0)),
            out_shape=pltpu.HBM(sent.shape, sent.dtype),
            compiler_params=params(1),
            cost_estimate=cost(20 * math.prod(sent.shape), field, sent),
            name="spread",
        )(*operands)

    def run_first(layers, got, pieces):
        count = len(layers)
        shapes = [f32(metals, count, part, modes, width), f32(metals, count, 2, modes, width)]
        shapes += [f32(metals, count // pieces, part, modes, width)] * pieces
        return pl.pallas_call(
            functools.partial(first_kernel, layers),
            grid=(metals,),
            in_specs=[
                pl.BlockSpec((blocks, 1) + got.shape[2:], lambda m: (0, m, 0, 0, 0, 0)),
                by_metal(weights),
                whole(cls),
            ],
            out_specs=[by_metal(s) for s in shapes],
            out_shape=[pltpu.HBM(s.shape, s.dtype) for s in shapes],
            compiler_params=params(1),
            cost_estimate=cost(300 * math.prod(got.shape), got, *shapes),
            name="first",
        )(got, weights, cls)

    def run_second(layers, g, low, high, l, beside, *halos):
        sent = f32(blocks, metals, each, len(layers), part, width)
        arrays = (g, low, high, l, beside, weights)
        return pl.pallas_call(
            functools.partial(second_kernel, layers),
            grid=(metals,),
            in_specs=[by_metal(a) for a in arrays]
            + [whole(cls), whole(vel), whole(disp)]
            + [by_metal(a) for a in halos],
            out_specs=pl.BlockSpec((blocks, 1) + sent.shape[2:], lambda m: (0, m, 0, 0, 0, 0)),
            out_shape=pltpu.HBM(sent.shape, sent.dtype),
            compiler_params=params(1),
            cost_estimate=cost(300 * math.prod(sent.shape), g, low, high, l, sent),
            name="second",
        )(*arrays, cls, vel, disp, *halos)

    def run_last(pair, got, *so_far):
        block = pl.BlockSpec((1, each, 2, rows, width), lambda m, k: (m, 0, pair(k), 0, 0))
        return pl.pallas_call(
            last_kernel,
            grid=(metals, 2),
            in_specs=[
                block,
                pl.BlockSpec((blocks, 1, each, 2, part, width), lambda m, k: (0, m, 0, k, 0, 0)),
            ]
            + [pl.BlockSpec(memory_space=pl.ANY)] * len(so_far),
            out_specs=block,
            out_shape=pltpu.HBM(field.shape, field.dtype),
            input_output_aliases={2: 0} if so_far else {},
            compiler_params=params(2),
            cost_estimate=cost(math.prod(got.shape), got, got, got),
            name="last",
        )(field, got, *so_far)

    lo = lax.ppermute(field[:, :, depth - 2 :], "space", up)
    hi = lax.ppermute(field[:, :, :2], "space", down)
    got_inner = over_modes(run_spread(inner))
    spread_outer = run_spread(outer, lo, hi)
    spread_outer, got_inner = after((spread_outer, got_inner))
    got_outer = over_modes(spread_outer)
    l_inner, beside_inner, g = run_first(inner, got_inner, 1)
    g, got_outer = after((g, got_outer))
    l_outer, beside_outer, low, high = run_first(outer, got_outer, 2)
    lo = lax.ppermute(high, "space", up)
    hi = lax.ppermute(low, "space", down)
    back_inner = over_modes(run_second(inner, g, low, high, l_inner, beside_inner))
    back_outer = run_second(outer, g, low, high, l_outer, beside_outer, lo, hi)
    back_outer, back_inner = after((back_outer, back_inner))
    back_outer = over_modes(back_outer)
    out = run_last(lambda k: k + 1, back_inner)
    return run_last(lambda k: 3 * k, back_outer, out)


def solution(mesh):
    in_specs = (
        P(None, "mode", "space", None, None),
        P("space", None, None),
        P("space", None, None),
        P(),
        P("space", None, None),
        P("space", None, None),
    )
    out_specs = P(None, "mode", "space", None, None)
    return jax.shard_map(
        on_device, mesh=mesh, in_specs=in_specs, out_specs=out_specs, check_vma=False
    )
```

```python
import functools
import math

import jax
import jax.numpy as jnp
import numpy as np
from jax import lax
from jax.experimental import pallas as pl
from jax.experimental.pallas import tpu as pltpu
from jax.sharding import PartitionSpec as P


TIME_STEP = 0.1
MOBILE_BASE = 0.7
RUN = 8
VMEM_LIMIT = 61 * 1024 * 1024


def legendre_weight(order):
    return math.comb(2 * order, order) / 4.0**order


def triple_table(terms_count):
    table = np.zeros((terms_count,) * 3, np.float64)
    for a in range(terms_count):
        for b in range(terms_count):
            for c in range(terms_count):
                total = a + b + c
                half = total // 2
                if total % 2 == 0 and max(a, b, c) <= half:
                    amount = legendre_weight(half - a) * legendre_weight(half - b) * legendre_weight(half - c)
                    amount = amount / legendre_weight(half) / (total + 1)
                    table[a, b, c] = amount * math.sqrt((2 * a + 1) * (2 * b + 1) * (2 * c + 1))
    return table.astype(np.float32)


def class_weights(mobility):
    metals, classes, modes = mobility.shape
    triple = jnp.asarray(triple_table(modes))
    mats = jnp.einsum("ijk,mck->mcij", triple, mobility, precision=lax.Precision.HIGHEST)
    mats = TIME_STEP * (mats + MOBILE_BASE * jnp.eye(modes, dtype=jnp.float32))
    mats = mats.reshape(metals, classes * modes, modes)
    high = lax.reduce_precision(mats, exponent_bits=8, mantissa_bits=7)
    return jnp.concatenate([high, high, mats - high], axis=2).astype(jnp.bfloat16)


def lane_neighbours(v):
    lane = lax.broadcasted_iota(jnp.int32, v.shape, v.ndim - 1)
    size = v.shape[-1]
    lower = jnp.where(lane == 0, 0.0, pltpu.roll(v, 1, v.ndim - 1))
    upper = jnp.where(lane == size - 1, 0.0, pltpu.roll(v, size - 1, v.ndim - 1))
    return lower + upper


def combine(l2, l1, mid, r1, r2, sides, vel, disp):
    spread = (16.0 / 12.0) * (l1 + r1) - (1.0 / 12.0) * (l2 + r2) - 6.5 * mid + sides
    carried = (1.0 / 3.0) * r1 + 0.5 * mid - l1 + (1.0 / 6.0) * l2
    return disp * spread - vel * carried


def spread_kernel(layers, f_ref, vel_ref, disp_ref, *rest):
    lo_ref, hi_ref, around_ref, ends_ref = rest[:4] if len(rest) == 5 else (None,) * 4
    out_ref = rest[-1]
    depth, rows, width = f_ref.shape[2:]
    blocks = out_ref.shape[0]
    part = rows // blocks
    count = len(layers)
    row = lax.broadcasted_iota(jnp.int32, (rows, width), 0)

    def layer(e, x):
        if x < 0:
            return lo_ref[0, e, x + 2] + ends_ref[0] * around_ref[0, e, x + 2]
        if x >= depth:
            return hi_ref[0, e, x - depth] + ends_ref[1] * around_ref[0, e, x - depth]
        return f_ref[0, e, x]

    zero_row = jnp.zeros((1, width), jnp.float32)
    for e in range(f_ref.shape[1]):
        for i, x in enumerate(layers):
            mid = layer(e, x)
            sides = lane_neighbours(mid)
            sides += jnp.where(row == 0, 0.0, pltpu.roll(mid, 1, 0))
            sides += jnp.where(row == rows - 1, 0.0, pltpu.roll(mid, rows - 1, 0))
            around = [layer(e, x + k) for k in (-2, -1, 0, 1, 2)]
            value = combine(*around, sides, vel_ref[x], disp_ref[x])
            for b in range(blocks):
                out_ref[b, 0, e, i] = value[b * part : (b + 1) * part]
                below = value[b * part - 1 : b * part] if b else zero_row
                above = value[(b + 1) * part : (b + 1) * part + 1] if b < blocks - 1 else zero_row
                out_ref[b, 0, e, count, i : i + 1] = below
                out_ref[b, 0, e, count, count + i : count + i + 1] = above


def couple(value, weights, classes, cls_row):
    modes, width = value.shape
    high = value.astype(jnp.bfloat16)
    low = (value - high.astype(jnp.float32)).astype(jnp.bfloat16)
    stacked = jnp.concatenate([high, low, high], axis=0)
    mixed = jnp.dot(weights, stacked, preferred_element_type=jnp.float32)
    picked = jnp.broadcast_to(cls_row, (modes, width))
    total = jnp.zeros((modes, width), jnp.float32)
    for c in range(classes):
        total = jnp.where(picked == c, mixed[c * modes : (c + 1) * modes], total)
    return total


def first_kernel(layers, r_ref, w_ref, cls_ref, l_ref, beside_ref, *g_refs):
    sources, _, each, slots, part, width = r_ref.shape
    modes = sources * each
    count = len(layers)
    share = count // len(g_refs)
    classes = w_ref.shape[1] // modes
    weights = w_ref[0]
    for s in range(slots):
        values = jnp.swapaxes(r_ref[:, 0, :, s].reshape(modes, part, width), 0, 1)
        for y in range(part):
            if s < count:
                x, row = layers[s], y + 1
            else:
                x, row = layers[y % count], (part + 1) * (y // count)
            got = couple(values[y], weights, classes, cls_ref[x, row : row + 1])
            if s < count:
                l_ref[0, s, y] = values[y]
                g_refs[s // share][0, s % share, y] = got
            else:
                beside_ref[0, y % count, y // count] = got


def second_kernel(layers, g_ref, low_ref, high_ref, l_ref, beside_ref, w_ref, cls_ref, vel_ref, disp_ref, *rest):
    lo_ref, hi_ref, around_ref, ends_ref = rest[:4] if len(rest) == 5 else (None,) * 4
    out_ref = rest[-1]
    inner, part, modes, width = g_ref.shape[1:]
    depth = inner + 4
    targets, _, each = out_ref.shape[:3]
    classes = w_ref.shape[1] // modes
    weights = w_ref[0]

    def at(x, y):
        if x < 0:
            return lo_ref[0, x + 2, y] + ends_ref[0] * around_ref[0, x + 2, y]
        if x < 2:
            return low_ref[0, x, y]
        if x < depth - 2:
            return g_ref[0, x - 2, y]
        if x < depth:
            return high_ref[0, x - depth + 2, y]
        return hi_ref[0, x - depth, y] + ends_ref[1] * around_ref[0, x - depth, y]

    for i, x in enumerate(layers):
        rows = []
        for y in range(part):
            mid = at(x, y)
            below = at(x, y - 1) if y else beside_ref[0, i, 0]
            above = at(x, y + 1) if y < part - 1 else beside_ref[0, i, 1]
            sides = lane_neighbours(mid) + (below + above)
            vel = jnp.broadcast_to(vel_ref[x, y : y + 1], (modes, width))
            disp = jnp.broadcast_to(disp_ref[x, y : y + 1], (modes, width))
            value = combine(at(x - 2, y), at(x - 1, y), mid, at(x + 1, y), at(x + 2, y), sides, vel, disp)
            value += 2.0 * l_ref[0, i, y]
            rows.append(couple(value, weights, classes, cls_ref[x, y + 1 : y + 2]))
        out_ref[:, 0, :, i] = jnp.swapaxes(jnp.stack(rows), 0, 1).reshape(targets, each, part, width)


def last_kernel(f_ref, r_ref, *rest):
    out_ref = rest[-1]
    blocks = r_ref.shape[0]
    part = r_ref.shape[4]
    for b in range(blocks):
        rows = slice(b * part, (b + 1) * part)
        out_ref[0, :, :, rows] = f_ref[0, :, :, rows] + r_ref[b, 0]


def staged(body, steps, inputs, outputs, flops, name, scalars=(), so_far=()):
    n_in, n_out = len(inputs), len(outputs)

    def kernel(*refs):
        in_refs, refs = refs[:n_in], refs[n_in:]
        scalar_refs, refs = refs[: len(scalars)], refs[len(scalars) :]
        refs = refs[len(so_far) :]
        out_refs, refs = refs[:n_out], refs[n_out:]
        in_bufs, out_bufs, (sems,) = refs[:n_in], refs[n_in : n_in + n_out], refs[n_in + n_out :]

        def load(k, i):
            index = inputs[k][2]
            if index is None:
                return pltpu.make_async_copy(in_refs[k], in_bufs[k], sems.at[k, 0])
            return pltpu.make_async_copy(in_refs[k].at[index(i)], in_bufs[k].at[i], sems.at[k, i])

        def store(k, i):
            return pltpu.make_async_copy(out_bufs[k].at[i], out_refs[k].at[outputs[k][2](i)], sems.at[n_in + k, i])

        for i in range(steps):
            for k in range(n_in):
                if i == 0 or inputs[k][2] is not None:
                    load(k, i).start()
        for k in range(n_in):
            if inputs[k][2] is None:
                load(k, 0).wait()

        def step(i, carry):
            for k in range(n_in):
                if inputs[k][2] is not None:
                    load(k, i).wait()
            blocks = [buf if spec[2] is None else buf.at[i] for buf, spec in zip(in_bufs, inputs)]
            body(*blocks, *scalar_refs, *[buf.at[i] for buf in out_bufs])
            for k in range(n_out):
                store(k, i).start()
            return carry

        lax.fori_loop(0, steps, step, 0)
        for i in range(steps):
            for k in range(n_out):
                store(k, i).wait()

    hbm = pl.BlockSpec(memory_space=pltpu.HBM)
    scratch = [
        pltpu.VMEM(block if index is None else (steps,) + block, array.dtype) for array, block, index in inputs
    ]
    scratch += [pltpu.VMEM((steps,) + block, shape.dtype) for shape, block, _ in outputs]
    moved = sum(4 * math.prod(a.shape) for a, *_ in (*inputs, *outputs))
    return pl.pallas_call(
        kernel,
        in_specs=[hbm] * n_in + [pl.BlockSpec(memory_space=pltpu.SMEM)] * len(scalars) + [hbm] * len(so_far),
        out_specs=[hbm] * n_out,
        out_shape=[pltpu.HBM(shape.shape, shape.dtype) for shape, *_ in outputs],
        scratch_shapes=scratch + [pltpu.SemaphoreType.DMA((n_in + n_out, steps))],
        input_output_aliases={n_in + len(scalars): 0} if so_far else {},
        compiler_params=pltpu.CompilerParams(vmem_limit_bytes=VMEM_LIMIT),
        cost_estimate=pl.CostEstimate(flops=flops, bytes_accessed=moved, transcendentals=0),
        name=name,
    )(*[array for array, *_ in inputs], *scalars, *so_far)


def halo_routes(space, blocks):
    direct, leave, arrive = [], [], []
    for s in range(space - 1):
        for m in range(blocks):
            ends = (s * blocks + m, (s + 1) * blocks + m)
            if (s + 1) % RUN or m < blocks // 2:
                direct.append(ends)
            else:
                near = (s + 2 - RUN) * blocks + m
                far = (s + RUN - 1) * blocks + m
                leave += [(ends[0], near), (ends[1], far)]
                arrive += [(near, ends[1]), (far, ends[0])]
    return direct, leave, arrive


def on_device(field, velocity, dispersion, mobility, material, fixed_mask):
    metals, each, depth, rows, width = field.shape
    modes = mobility.shape[2]
    classes = mobility.shape[1]
    blocks = lax.axis_size("mode")
    part = rows // blocks
    space = lax.axis_size("space")
    direct, leave, arrive = halo_routes(space, blocks)
    back = [(b, a) for a, b in direct]
    both = ("space", "mode")
    place = lax.axis_index("space") % RUN
    ends = jnp.stack([place == 0, place == RUN - 1]).astype(jnp.float32)

    def exchange(low, high):
        lo = lax.ppermute(high, both, direct)
        hi = lax.ppermute(low, both, back)
        around = lax.ppermute(jnp.where(place == RUN - 1, high, low), both, leave)
        return lo, hi, lax.ppermute(around, both, arrive), ends

    inner = tuple(range(2, depth - 2))
    outer = (0, 1, depth - 2, depth - 1)
    after = lax.optimization_barrier

    weights = class_weights(mobility)
    here = lax.axis_index("mode") * part
    cls = jnp.where(fixed_mask == 1, classes, material)
    cls = lax.dynamic_slice_in_dim(jnp.pad(cls, ((0, 0), (1, 1), (0, 0))), here, part + 2, 1)
    vel = lax.dynamic_slice_in_dim(velocity, here, part, 1)
    disp = lax.dynamic_slice_in_dim(dispersion, here, part, 1)

    def f32(*shape):
        return jax.ShapeDtypeStruct(shape, jnp.float32)

    def by_metal(array):
        return array, (1,) + array.shape[1:], lambda i: pl.ds(i, 1)

    def by_unit(array):
        return array, (array.shape[0], 1) + array.shape[2:], lambda i: (slice(None), pl.ds(i, 1))

    def whole(array):
        return array, array.shape, None

    def over_modes(array):
        return lax.all_to_all(array, "mode", split_axis=0, concat_axis=0, tiled=True)

    def run_spread(layers, *halos):
        sent = f32(blocks, metals, each, len(layers) + 1, part, width)
        (out,) = staged(
            functools.partial(spread_kernel, layers),
            metals,
            [by_metal(field), whole(velocity), whole(dispersion)] + [by_metal(h) for h in halos[:3]],
            [by_unit(sent)],
            20 * math.prod(sent.shape),
            "spread",
            halos[3:],
        )
        return out

    def run_first(layers, got, pieces):
        count = len(layers)
        shapes = [f32(metals, count, part, modes, width), f32(metals, count, 2, modes, width)]
        shapes += [f32(metals, count // pieces, part, modes, width)] * pieces
        return staged(
            functools.partial(first_kernel, layers),
            metals,
            [by_unit(got), by_metal(weights), whole(cls)],
            [by_metal(s) for s in shapes],
            300 * math.prod(got.shape),
            "first",
        )

    def run_second(layers, g, low, high, l, beside, *halos):
        sent = f32(blocks, metals, each, len(layers), part, width)
        (out,) = staged(
            functools.partial(second_kernel, layers),
            metals,
            [by_metal(a) for a in (g, low, high, l, beside, weights)]
            + [whole(cls), whole(vel), whole(disp)]
            + [by_metal(a) for a in halos[:3]],
            [by_unit(sent)],
            300 * math.prod(sent.shape),
            "second",
            halos[3:],
        )
        return out

    def run_last(pair, got, *so_far):
        block = (1, each, 2, rows, width)

        def at(i):
            return pl.ds(i // 2, 1), slice(None), pl.ds(2 * pair(i % 2), 2)

        (out,) = staged(
            last_kernel,
            2 * metals,
            [
                (field, block, at),
                (
                    got,
                    (blocks, 1, each, 2, part, width),
                    lambda i: (slice(None), pl.ds(i // 2, 1), slice(None), pl.ds(2 * (i % 2), 2)),
                ),
            ],
            [(field, block, at)],
            math.prod(got.shape),
            "last",
            so_far=so_far,
        )
        return out

    sides = exchange(field[:, :, :2], field[:, :, depth - 2 :])
    got_inner = over_modes(run_spread(inner))
    spread_outer = run_spread(outer, *sides)
    spread_outer, got_inner = after((spread_outer, got_inner))
    got_outer = over_modes(spread_outer)
    l_inner, beside_inner, g = run_first(inner, got_inner, 1)
    g, got_outer = after((g, got_outer))
    l_outer, beside_outer, low, high = run_first(outer, got_outer, 2)
    sides = exchange(low, high)
    back_inner = over_modes(run_second(inner, g, low, high, l_inner, beside_inner))
    back_outer = run_second(outer, g, low, high, l_outer, beside_outer, *sides)
    back_outer, back_inner = after((back_outer, back_inner))
    back_outer = over_modes(back_outer)
    out = run_last(lambda k: k + 1, back_inner)
    return run_last(lambda k: 3 * k, back_outer, out)


def solution(mesh):
    in_specs = (
        P(None, "mode", "space", None, None),
        P("space", None, None),
        P("space", None, None),
        P(),
        P("space", None, None),
        P("space", None, None),
    )
    out_specs = P(None, "mode", "space", None, None)
    return jax.shard_map(
        on_device, mesh=mesh, in_specs=in_specs, out_specs=out_specs, check_vma=False
    )
```

```python
import functools
import math

import jax
import jax.numpy as jnp
import numpy as np
from jax import lax
from jax.experimental import pallas as pl
from jax.experimental.pallas import tpu as pltpu
from jax.sharding import PartitionSpec as P


TIME_STEP = 0.1
MOBILE_BASE = 0.7
RUN = 8
RELAYS = (((5, 2), (2, 5)), ((6, 1), (1, 6)))
SHARED_LIMIT = 50 * 1024 * 1024
VMEM_LIMIT = 61 * 1024 * 1024


def legendre_weight(order):
    return math.comb(2 * order, order) / 4.0**order


def triple_table(terms_count):
    table = np.zeros((terms_count,) * 3, np.float64)
    for a in range(terms_count):
        for b in range(terms_count):
            for c in range(terms_count):
                total = a + b + c
                half = total // 2
                if total % 2 == 0 and max(a, b, c) <= half:
                    amount = legendre_weight(half - a) * legendre_weight(half - b) * legendre_weight(half - c)
                    amount = amount / legendre_weight(half) / (total + 1)
                    table[a, b, c] = amount * math.sqrt((2 * a + 1) * (2 * b + 1) * (2 * c + 1))
    return table.astype(np.float32)


def class_weights(mobility):
    metals, classes, modes = mobility.shape
    triple = jnp.asarray(triple_table(modes))
    mats = jnp.einsum("ijk,mck->mcij", triple, mobility, precision=lax.Precision.HIGHEST)
    mats = TIME_STEP * (mats + MOBILE_BASE * jnp.eye(modes, dtype=jnp.float32))
    mats = mats.reshape(metals, classes * modes, modes)
    high = lax.reduce_precision(mats, exponent_bits=8, mantissa_bits=7)
    return jnp.concatenate([high, high, mats - high], axis=2).astype(jnp.bfloat16)


def lane_neighbours(v):
    lane = lax.broadcasted_iota(jnp.int32, v.shape, v.ndim - 1)
    size = v.shape[-1]
    lower = jnp.where(lane == 0, 0.0, pltpu.roll(v, 1, v.ndim - 1))
    upper = jnp.where(lane == size - 1, 0.0, pltpu.roll(v, size - 1, v.ndim - 1))
    return lower + upper


def combine(l2, l1, mid, r1, r2, sides, vel, disp):
    spread = (16.0 / 12.0) * (l1 + r1) - (1.0 / 12.0) * (l2 + r2) - 6.5 * mid + sides
    carried = (1.0 / 3.0) * r1 + 0.5 * mid - l1 + (1.0 / 6.0) * l2
    return disp * spread - vel * carried


def spread_kernel(layers, f_ref, vel_ref, disp_ref, *rest):
    lo_ref, hi_ref, *around_refs, ends_ref = rest[:5] if len(rest) == 6 else (None,) * 5
    out_ref = rest[-1]
    depth, rows, width = f_ref.shape[2:]
    blocks = out_ref.shape[0]
    part = rows // blocks
    count = len(layers)
    row = lax.broadcasted_iota(jnp.int32, (rows, width), 0)

    def layer(e, x):
        if x < 0:
            return lo_ref[0, e, x + 2] + ends_ref[0] * around_refs[x + 2][0, e, 0]
        if x >= depth:
            return hi_ref[0, e, x - depth] + ends_ref[1] * around_refs[x - depth][0, e, 0]
        return f_ref[0, e, x]

    zero_row = jnp.zeros((1, width), jnp.float32)
    for e in range(f_ref.shape[1]):
        for i, x in enumerate(layers):
            mid = layer(e, x)
            sides = lane_neighbours(mid)
            sides += jnp.where(row == 0, 0.0, pltpu.roll(mid, 1, 0))
            sides += jnp.where(row == rows - 1, 0.0, pltpu.roll(mid, rows - 1, 0))
            around = [layer(e, x + k) for k in (-2, -1, 0, 1, 2)]
            value = combine(*around, sides, vel_ref[x], disp_ref[x])
            for b in range(blocks):
                out_ref[b, 0, e, i] = value[b * part : (b + 1) * part]
                below = value[b * part - 1 : b * part] if b else zero_row
                above = value[(b + 1) * part : (b + 1) * part + 1] if b < blocks - 1 else zero_row
                out_ref[b, 0, e, count, i : i + 1] = below
                out_ref[b, 0, e, count, count + i : count + i + 1] = above


def couple(value, weights, classes, cls_row):
    modes, width = value.shape
    high = value.astype(jnp.bfloat16)
    low = (value - high.astype(jnp.float32)).astype(jnp.bfloat16)
    stacked = jnp.concatenate([high, low, high], axis=0)
    mixed = jnp.dot(weights, stacked, preferred_element_type=jnp.float32)
    picked = jnp.broadcast_to(cls_row, (8, width))
    totals = [jnp.zeros((8, width), jnp.float32)] * (modes // 8)
    for c in range(classes):
        here = picked == c
        for k in range(modes // 8):
            at = c * modes + 8 * k
            totals[k] = jnp.where(here, mixed[at : at + 8], totals[k])
    return jnp.concatenate(totals, axis=0)


def first_kernel(layers, r_ref, w_ref, cls_ref, l_ref, beside_ref, *g_refs):
    sources, _, each, slots, part, width = r_ref.shape
    modes = sources * each
    count = len(layers)
    share = count // len(g_refs)
    classes = w_ref.shape[1] // modes
    weights = w_ref[0]
    for s in range(slots):
        values = jnp.swapaxes(r_ref[:, 0, :, s].reshape(modes, part, width), 0, 1)
        for y in range(part):
            if s < count:
                x, row = layers[s], y + 1
            else:
                x, row = layers[y % count], (part + 1) * (y // count)
            got = couple(values[y], weights, classes, cls_ref[x, row : row + 1])
            if s < count:
                l_ref[0, s, y] = values[y]
                g_refs[s // share][0, s % share, y] = got
            else:
                beside_ref[0, y % count, y // count] = got


def second_kernel(layers, g_ref, low_ref, high_ref, l_ref, beside_ref, w_ref, cls_ref, vel_ref, disp_ref, *rest):
    lo_ref, hi_ref, *around_refs, ends_ref = rest[:5] if len(rest) == 6 else (None,) * 5
    out_ref = rest[-1]
    inner, part, modes, width = g_ref.shape[1:]
    depth = inner + 4
    targets, _, each = out_ref.shape[:3]
    classes = w_ref.shape[1] // modes
    weights = w_ref[0]

    def at(x, y):
        if x < 0:
            return lo_ref[0, x + 2, y] + ends_ref[0] * around_refs[x + 2][0, 0, y]
        if x < 2:
            return low_ref[0, x, y]
        if x < depth - 2:
            return g_ref[0, x - 2, y]
        if x < depth:
            return high_ref[0, x - depth + 2, y]
        return hi_ref[0, x - depth, y] + ends_ref[1] * around_refs[x - depth][0, 0, y]

    for i, x in enumerate(layers):
        rows = []
        for y in range(part):
            mid = at(x, y)
            below = at(x, y - 1) if y else beside_ref[0, i, 0]
            above = at(x, y + 1) if y < part - 1 else beside_ref[0, i, 1]
            sides = lane_neighbours(mid) + (below + above)
            vel = jnp.broadcast_to(vel_ref[x, y : y + 1], (modes, width))
            disp = jnp.broadcast_to(disp_ref[x, y : y + 1], (modes, width))
            value = combine(at(x - 2, y), at(x - 1, y), mid, at(x + 1, y), at(x + 2, y), sides, vel, disp)
            value += 2.0 * l_ref[0, i, y]
            rows.append(couple(value, weights, classes, cls_ref[x, y + 1 : y + 2]))
        out_ref[:, 0, :, i] = jnp.swapaxes(jnp.stack(rows), 0, 1).reshape(targets, each, part, width)


def last_kernel(f_ref, r_ref, *rest):
    out_ref = rest[-1]
    blocks = r_ref.shape[0]
    part = r_ref.shape[4]
    for b in range(blocks):
        rows = slice(b * part, (b + 1) * part)
        out_ref[0, :, :, rows] = f_ref[0, :, :, rows] + r_ref[b, 0]


def staged(body, steps, inputs, outputs, flops, name, scalars=(), so_far=(), arrived=()):
    n_in, n_out = len(inputs), len(outputs)

    def kernel(*refs):
        in_refs, refs = refs[:n_in], refs[n_in:]
        scalar_refs, refs = refs[: len(scalars)], refs[len(scalars) :]
        refs = refs[len(so_far) :]
        out_refs, refs = refs[:n_out], refs[n_out:]
        in_bufs, out_bufs, (sems,) = refs[:n_in], refs[n_in : n_in + n_out], refs[n_in + n_out :]

        def load(k, i):
            index = inputs[k][2]
            if index is None:
                return pltpu.make_async_copy(in_refs[k], in_bufs[k], sems.at[k, 0])
            return pltpu.make_async_copy(in_refs[k].at[index(i)], in_bufs[k].at[i], sems.at[k, i])

        def store(k, i):
            return pltpu.make_async_copy(out_bufs[k].at[i], out_refs[k].at[outputs[k][2](i)], sems.at[n_in + k, i])

        for i in range(steps):
            for k in range(n_in):
                if i == 0 or inputs[k][2] is not None:
                    load(k, i).start()
        for k in range(n_in):
            if inputs[k][2] is None:
                load(k, 0).wait()

        def step(i, carry):
            for k in range(n_in):
                if inputs[k][2] is not None:
                    load(k, i).wait()
            blocks = [buf if spec[2] is None else buf.at[i] for buf, spec in zip(in_bufs, inputs)]
            body(*blocks, *scalar_refs, *[buf.at[i] for buf in out_bufs])
            for k in range(n_out):
                store(k, i).start()
            return carry

        lax.fori_loop(0, steps, step, 0)
        for i in range(steps):
            for k in range(n_out):
                store(k, i).wait()

    hbm = pl.BlockSpec(memory_space=pltpu.HBM)
    scratch = [
        pltpu.VMEM(block if index is None else (steps,) + block, array.dtype) for array, block, index in inputs
    ]
    scratch += [pltpu.VMEM((steps,) + block, shape.dtype) for shape, block, _ in outputs]
    moved = sum(4 * math.prod(a.shape) for a, *_ in (*inputs, *outputs))
    return pl.pallas_call(
        kernel,
        in_specs=[pl.BlockSpec(memory_space=pl.ANY) if k in arrived else hbm for k in range(n_in)]
        + [pl.BlockSpec(memory_space=pltpu.SMEM)] * len(scalars) + [hbm] * len(so_far),
        out_specs=[hbm] * n_out,
        out_shape=[pltpu.HBM(shape.shape, shape.dtype) for shape, *_ in outputs],
        scratch_shapes=scratch + [pltpu.SemaphoreType.DMA((n_in + n_out, steps))],
        input_output_aliases={n_in + len(scalars): 0} if so_far else {},
        compiler_params=pltpu.CompilerParams(vmem_limit_bytes=SHARED_LIMIT if arrived else VMEM_LIMIT),
        cost_estimate=pl.CostEstimate(flops=flops, bytes_accessed=moved, transcendentals=0),
        name=name,
    )(*[array for array, *_ in inputs], *scalars, *so_far)


def halo_routes(space, blocks):
    direct, relayed = [], [([], []), ([], [])]
    for s in range(space - 1):
        for m in range(blocks):
            ends = (s * blocks + m, (s + 1) * blocks + m)
            if (s + 1) % RUN:
                direct.append(ends)
                continue
            for (leave, arrive), relays in zip(relayed, RELAYS):
                up, down = relays[2 * m // blocks]
                near = (s + 1 - RUN + up) * blocks + m
                far = (s + 1 + down) * blocks + m
                leave += [(ends[0], near), (ends[1], far)]
                arrive += [(near, ends[1]), (far, ends[0])]
    return direct, relayed


def on_device(field, velocity, dispersion, mobility, material, fixed_mask):
    metals, each, depth, rows, width = field.shape
    modes = mobility.shape[2]
    classes = mobility.shape[1]
    blocks = lax.axis_size("mode")
    part = rows // blocks
    space = lax.axis_size("space")
    direct, relayed = halo_routes(space, blocks)
    back = [(b, a) for a, b in direct]
    both = ("space", "mode")
    place = lax.axis_index("space") % RUN
    ends = jnp.stack([place == 0, place == RUN - 1]).astype(jnp.float32)

    def exchange(low, high, axis):
        lo = lax.ppermute(high, both, direct)
        hi = lax.ppermute(low, both, back)
        out = jnp.where(place == RUN - 1, high, low)
        around = []
        for layer, (leave, arrive) in enumerate(relayed):
            piece = lax.slice_in_dim(out, layer, layer + 1, axis=axis)
            around.append(lax.ppermute(lax.ppermute(piece, both, leave), both, arrive))
        return lo, hi, *around, ends

    inner = tuple(range(2, depth - 2))
    outer = (0, 1, depth - 2, depth - 1)
    after = lax.optimization_barrier

    weights = class_weights(mobility)
    here = lax.axis_index("mode") * part
    cls = jnp.where(fixed_mask == 1, classes, material)
    cls = lax.dynamic_slice_in_dim(jnp.pad(cls, ((0, 0), (1, 1), (0, 0))), here, part + 2, 1)
    vel = lax.dynamic_slice_in_dim(velocity, here, part, 1)
    disp = lax.dynamic_slice_in_dim(dispersion, here, part, 1)

    def f32(*shape):
        return jax.ShapeDtypeStruct(shape, jnp.float32)

    def by_metal(array):
        return array, (1,) + array.shape[1:], lambda i: pl.ds(i, 1)

    def by_unit(array):
        return array, (array.shape[0], 1) + array.shape[2:], lambda i: (slice(None), pl.ds(i, 1))

    def whole(array):
        return array, array.shape, None

    def over_modes(array):
        return lax.all_to_all(array, "mode", split_axis=0, concat_axis=0, tiled=True)

    def run_spread(layers, *halos):
        sent = f32(blocks, metals, each, len(layers) + 1, part, width)
        (out,) = staged(
            functools.partial(spread_kernel, layers),
            metals,
            [by_metal(field), whole(velocity), whole(dispersion)] + [by_metal(h) for h in halos[:4]],
            [by_unit(sent)],
            20 * math.prod(sent.shape),
            "spread",
            halos[4:],
            arrived=(3, 4, 5, 6) if halos else (),
        )
        return out

    def run_first(layers, got, pieces):
        count = len(layers)
        shapes = [f32(metals, count, part, modes, width), f32(metals, count, 2, modes, width)]
        shapes += [f32(metals, count // pieces, part, modes, width)] * pieces
        return staged(
            functools.partial(first_kernel, layers),
            metals,
            [by_unit(got), by_metal(weights), whole(cls)],
            [by_metal(s) for s in shapes],
            300 * math.prod(got.shape),
            "first",
            arrived=(0,),
        )

    def run_second(layers, g, low, high, l, beside, *halos):
        sent = f32(blocks, metals, each, len(layers), part, width)
        (out,) = staged(
            functools.partial(second_kernel, layers),
            metals,
            [by_metal(a) for a in (g, low, high, l, beside, weights)]
            + [whole(cls), whole(vel), whole(disp)]
            + [by_metal(a) for a in halos[:4]],
            [by_unit(sent)],
            300 * math.prod(sent.shape),
            "second",
            halos[4:],
            arrived=(9, 10, 11, 12) if halos else (),
        )
        return out

    def run_last(pair, got, *so_far):
        block = (1, each, 2, rows, width)

        def at(i):
            return pl.ds(i // 2, 1), slice(None), pl.ds(2 * pair(i % 2), 2)

        (out,) = staged(
            last_kernel,
            2 * metals,
            [
                (field, block, at),
                (
                    got,
                    (blocks, 1, each, 2, part, width),
                    lambda i: (slice(None), pl.ds(i // 2, 1), slice(None), pl.ds(2 * (i % 2), 2)),
                ),
            ],
            [(field, block, at)],
            math.prod(got.shape),
            "last",
            so_far=so_far,
            arrived=(1,),
        )
        return out

    sides = exchange(field[:, :, :2], field[:, :, depth - 2 :], 2)
    got_inner = over_modes(run_spread(inner))
    spread_outer = run_spread(outer, *sides)
    spread_outer, got_inner = after((spread_outer, got_inner))
    got_outer = over_modes(spread_outer)
    l_inner, beside_inner, g = run_first(inner, got_inner, 1)
    g, got_outer = after((g, got_outer))
    l_outer, beside_outer, low, high = run_first(outer, got_outer, 2)
    sides = exchange(low, high, 1)
    back_inner = over_modes(run_second(inner, g, low, high, l_inner, beside_inner))
    back_outer = run_second(outer, g, low, high, l_outer, beside_outer, *sides)
    back_outer, back_inner = after((back_outer, back_inner))
    back_outer = over_modes(back_outer)
    out = run_last(lambda k: k + 1, back_inner)
    return run_last(lambda k: 3 * k, back_outer, out)


def solution(mesh):
    in_specs = (
        P(None, "mode", "space", None, None),
        P("space", None, None),
        P("space", None, None),
        P(),
        P("space", None, None),
        P("space", None, None),
    )
    out_specs = P(None, "mode", "space", None, None)
    return jax.shard_map(
        on_device, mesh=mesh, in_specs=in_specs, out_specs=out_specs, check_vma=False
    )
```

```python
import functools
import math

import jax
import jax.numpy as jnp
import numpy as np
from jax import lax
from jax.experimental import pallas as pl
from jax.experimental.pallas import tpu as pltpu
from jax.sharding import PartitionSpec as P


TIME_STEP = 0.1
MOBILE_BASE = 0.7
RUN = 8
RELAYS = (((6, 1), (1, 6)), ((5, 2), (2, 5)))
SHARED_LIMIT = 50 * 1024 * 1024
VMEM_LIMIT = 61 * 1024 * 1024


def legendre_weight(order):
    return math.comb(2 * order, order) / 4.0**order


def triple_table(terms_count):
    table = np.zeros((terms_count,) * 3, np.float64)
    for a in range(terms_count):
        for b in range(terms_count):
            for c in range(terms_count):
                total = a + b + c
                half = total // 2
                if total % 2 == 0 and max(a, b, c) <= half:
                    amount = legendre_weight(half - a) * legendre_weight(half - b) * legendre_weight(half - c)
                    amount = amount / legendre_weight(half) / (total + 1)
                    table[a, b, c] = amount * math.sqrt((2 * a + 1) * (2 * b + 1) * (2 * c + 1))
    return table.astype(np.float32)


def class_weights(mobility):
    metals, classes, modes = mobility.shape
    triple = jnp.asarray(triple_table(modes))
    mats = jnp.einsum("ijk,mck->mcij", triple, mobility, precision=lax.Precision.HIGHEST)
    mats = TIME_STEP * (mats + MOBILE_BASE * jnp.eye(modes, dtype=jnp.float32))
    mats = mats.reshape(metals, classes * modes, modes)
    high = lax.reduce_precision(mats, exponent_bits=8, mantissa_bits=7)
    return jnp.concatenate([high, high, mats - high], axis=2).astype(jnp.bfloat16)


def lane_neighbours(v):
    lane = lax.broadcasted_iota(jnp.int32, v.shape, v.ndim - 1)
    size = v.shape[-1]
    lower = jnp.where(lane == 0, 0.0, pltpu.roll(v, 1, v.ndim - 1))
    upper = jnp.where(lane == size - 1, 0.0, pltpu.roll(v, size - 1, v.ndim - 1))
    return lower + upper


def combine(l2, l1, mid, r1, r2, sides, vel, disp):
    spread = (16.0 / 12.0) * (l1 + r1) - (1.0 / 12.0) * (l2 + r2) - 6.5 * mid + sides
    carried = (1.0 / 3.0) * r1 + 0.5 * mid - l1 + (1.0 / 6.0) * l2
    return disp * spread - vel * carried


def spread_kernel(layers, f_ref, vel_ref, disp_ref, *rest):
    lo_ref, hi_ref, *around_refs, ends_ref = rest[:5] if len(rest) == 6 else (None,) * 5
    out_ref = rest[-1]
    depth, rows, width = f_ref.shape[2:]
    blocks = out_ref.shape[0]
    part = rows // blocks
    count = len(layers)
    row = lax.broadcasted_iota(jnp.int32, (rows, width), 0)

    def layer(e, x):
        if x < 0:
            return lo_ref[0, e, x + 2] + ends_ref[0] * around_refs[x + 2][0, e, 0]
        if x >= depth:
            return hi_ref[0, e, x - depth] + ends_ref[1] * around_refs[x - depth][0, e, 0]
        return f_ref[0, e, x]

    zero_row = jnp.zeros((1, width), jnp.float32)
    for e in range(f_ref.shape[1]):
        for i, x in enumerate(layers):
            mid = layer(e, x)
            sides = lane_neighbours(mid)
            sides += jnp.where(row == 0, 0.0, pltpu.roll(mid, 1, 0))
            sides += jnp.where(row == rows - 1, 0.0, pltpu.roll(mid, rows - 1, 0))
            around = [layer(e, x + k) for k in (-2, -1, 0, 1, 2)]
            value = combine(*around, sides, vel_ref[x], disp_ref[x])
            for b in range(blocks):
                out_ref[b, 0, e, i] = value[b * part : (b + 1) * part]
                below = value[b * part - 1 : b * part] if b else zero_row
                above = value[(b + 1) * part : (b + 1) * part + 1] if b < blocks - 1 else zero_row
                out_ref[b, 0, e, count, i : i + 1] = below
                out_ref[b, 0, e, count, count + i : count + i + 1] = above


def couple(value, weights, classes, cls_row):
    modes, width = value.shape
    high = value.astype(jnp.bfloat16)
    low = (value - high.astype(jnp.float32)).astype(jnp.bfloat16)
    stacked = jnp.concatenate([high, low, high], axis=0)
    mixed = jnp.dot(weights, stacked, preferred_element_type=jnp.float32)
    picked = jnp.broadcast_to(cls_row, (8, width))
    totals = [jnp.zeros((8, width), jnp.float32)] * (modes // 8)
    for c in range(classes):
        here = picked == c
        for k in range(modes // 8):
            at = c * modes + 8 * k
            totals[k] = jnp.where(here, mixed[at : at + 8], totals[k])
    return jnp.concatenate(totals, axis=0)


def first_kernel(layers, r_ref, w_ref, cls_ref, l_ref, beside_ref, *g_refs):
    sources, _, each, slots, part, width = r_ref.shape
    modes = sources * each
    count = len(layers)
    share = count // len(g_refs)
    classes = w_ref.shape[1] // modes
    weights = w_ref[0]
    for s in range(slots):
        values = jnp.swapaxes(r_ref[:, 0, :, s].reshape(modes, part, width), 0, 1)
        for y in range(part):
            if s < count:
                x, row = layers[s], y + 1
            else:
                x, row = layers[y % count], (part + 1) * (y // count)
            got = couple(values[y], weights, classes, cls_ref[x, row : row + 1])
            if s < count:
                l_ref[0, s, y] = values[y]
                g_refs[s // share][0, s % share, y] = got
            else:
                beside_ref[0, y % count, y // count] = got


def second_kernel(layers, g_ref, low_ref, high_ref, l_ref, beside_ref, w_ref, cls_ref, vel_ref, disp_ref, *rest):
    lo_ref, hi_ref, *around_refs, ends_ref = rest[:5] if len(rest) == 6 else (None,) * 5
    out_ref = rest[-1]
    inner, part, modes, width = g_ref.shape[1:]
    depth = inner + 4
    targets, _, each = out_ref.shape[:3]
    classes = w_ref.shape[1] // modes
    weights = w_ref[0]

    def at(x, y):
        if x < 0:
            return lo_ref[0, x + 2, y] + ends_ref[0] * around_refs[x + 2][0, 0, y]
        if x < 2:
            return low_ref[0, x, y]
        if x < depth - 2:
            return g_ref[0, x - 2, y]
        if x < depth:
            return high_ref[0, x - depth + 2, y]
        return hi_ref[0, x - depth, y] + ends_ref[1] * around_refs[x - depth][0, 0, y]

    for i, x in enumerate(layers):
        rows = []
        for y in range(part):
            mid = at(x, y)
            below = at(x, y - 1) if y else beside_ref[0, i, 0]
            above = at(x, y + 1) if y < part - 1 else beside_ref[0, i, 1]
            sides = lane_neighbours(mid) + (below + above)
            vel = jnp.broadcast_to(vel_ref[x, y : y + 1], (modes, width))
            disp = jnp.broadcast_to(disp_ref[x, y : y + 1], (modes, width))
            value = combine(at(x - 2, y), at(x - 1, y), mid, at(x + 1, y), at(x + 2, y), sides, vel, disp)
            value += 2.0 * l_ref[0, i, y]
            rows.append(couple(value, weights, classes, cls_ref[x, y + 1 : y + 2]))
        out_ref[:, 0, :, i] = jnp.swapaxes(jnp.stack(rows), 0, 1).reshape(targets, each, part, width)


def last_kernel(f_ref, r_ref, *rest):
    out_ref = rest[-1]
    blocks = r_ref.shape[0]
    part = r_ref.shape[4]
    for b in range(blocks):
        rows = slice(b * part, (b + 1) * part)
        out_ref[0, :, :, rows] = f_ref[0, :, :, rows] + r_ref[b, 0]


def staged(body, steps, inputs, outputs, flops, name, scalars=(), so_far=(), arrived=(), limit=SHARED_LIMIT):
    n_in, n_out = len(inputs), len(outputs)

    def kernel(*refs):
        in_refs, refs = refs[:n_in], refs[n_in:]
        scalar_refs, refs = refs[: len(scalars)], refs[len(scalars) :]
        refs = refs[len(so_far) :]
        out_refs, refs = refs[:n_out], refs[n_out:]
        in_bufs, out_bufs, (sems,) = refs[:n_in], refs[n_in : n_in + n_out], refs[n_in + n_out :]

        def load(k, i):
            index = inputs[k][2]
            if index is None:
                return pltpu.make_async_copy(in_refs[k], in_bufs[k], sems.at[k, 0])
            return pltpu.make_async_copy(in_refs[k].at[index(i)], in_bufs[k].at[i], sems.at[k, i])

        def store(k, i):
            return pltpu.make_async_copy(out_bufs[k].at[i], out_refs[k].at[outputs[k][2](i)], sems.at[n_in + k, i])

        for i in range(steps):
            for k in range(n_in):
                if i == 0 or inputs[k][2] is not None:
                    load(k, i).start()
        for k in range(n_in):
            if inputs[k][2] is None:
                load(k, 0).wait()

        def step(i, carry):
            for k in range(n_in):
                if inputs[k][2] is not None:
                    load(k, i).wait()
            blocks = [buf if spec[2] is None else buf.at[i] for buf, spec in zip(in_bufs, inputs)]
            body(*blocks, *scalar_refs, *[buf.at[i] for buf in out_bufs])
            for k in range(n_out):
                store(k, i).start()
            return carry

        lax.fori_loop(0, steps, step, 0)
        for i in range(steps):
            for k in range(n_out):
                store(k, i).wait()

    hbm = pl.BlockSpec(memory_space=pltpu.HBM)
    scratch = [
        pltpu.VMEM(block if index is None else (steps,) + block, array.dtype) for array, block, index in inputs
    ]
    scratch += [pltpu.VMEM((steps,) + block, shape.dtype) for shape, block, _ in outputs]
    moved = sum(4 * math.prod(a.shape) for a, *_ in (*inputs, *outputs))
    return pl.pallas_call(
        kernel,
        in_specs=[pl.BlockSpec(memory_space=pl.ANY) if k in arrived else hbm for k in range(n_in)]
        + [pl.BlockSpec(memory_space=pltpu.SMEM)] * len(scalars) + [hbm] * len(so_far),
        out_specs=[hbm] * n_out,
        out_shape=[pltpu.HBM(shape.shape, shape.dtype) for shape, *_ in outputs],
        scratch_shapes=scratch + [pltpu.SemaphoreType.DMA((n_in + n_out, steps))],
        input_output_aliases={n_in + len(scalars): 0} if so_far else {},
        compiler_params=pltpu.CompilerParams(vmem_limit_bytes=limit if arrived else VMEM_LIMIT),
        cost_estimate=pl.CostEstimate(flops=flops, bytes_accessed=moved, transcendentals=0),
        name=name,
    )(*[array for array, *_ in inputs], *scalars, *so_far)


def halo_routes(space, blocks):
    direct, relayed = [], [([], []), ([], [])]
    for s in range(space - 1):
        for m in range(blocks):
            ends = (s * blocks + m, (s + 1) * blocks + m)
            if (s + 1) % RUN:
                direct.append(ends)
                continue
            for (leave, arrive), relays in zip(relayed, RELAYS):
                up, down = relays[2 * m // blocks]
                near = (s + 1 - RUN + up) * blocks + m
                far = (s + 1 + down) * blocks + m
                leave += [(ends[0], near), (ends[1], far)]
                arrive += [(near, ends[1]), (far, ends[0])]
    return direct, relayed


def on_device(field, velocity, dispersion, mobility, material, fixed_mask):
    metals, each, depth, rows, width = field.shape
    modes = mobility.shape[2]
    classes = mobility.shape[1]
    blocks = lax.axis_size("mode")
    part = rows // blocks
    space = lax.axis_size("space")
    direct, relayed = halo_routes(space, blocks)
    back = [(b, a) for a, b in direct]
    both = ("space", "mode")
    place = lax.axis_index("space") % RUN
    ends = jnp.stack([place == 0, place == RUN - 1]).astype(jnp.float32)

    def exchange(low, high, axis):
        lo = lax.ppermute(high, both, direct)
        hi = lax.ppermute(low, both, back)
        out = jnp.where(place == RUN - 1, high, low)
        around = []
        for layer, (leave, arrive) in enumerate(relayed):
            piece = lax.slice_in_dim(out, layer, layer + 1, axis=axis)
            around.append(lax.ppermute(lax.ppermute(piece, both, leave), both, arrive))
        return lo, hi, *around, ends

    inner = tuple(range(2, depth - 2))
    outer = (0, 1, depth - 2, depth - 1)
    after = lax.optimization_barrier

    weights = class_weights(mobility)
    here = lax.axis_index("mode") * part
    cls = jnp.where(fixed_mask == 1, classes, material)
    cls = lax.dynamic_slice_in_dim(jnp.pad(cls, ((0, 0), (1, 1), (0, 0))), here, part + 2, 1)
    vel = lax.dynamic_slice_in_dim(velocity, here, part, 1)
    disp = lax.dynamic_slice_in_dim(dispersion, here, part, 1)

    def f32(*shape):
        return jax.ShapeDtypeStruct(shape, jnp.float32)

    def by_metal(array):
        return array, (1,) + array.shape[1:], lambda i: pl.ds(i, 1)

    def by_unit(array):
        return array, (array.shape[0], 1) + array.shape[2:], lambda i: (slice(None), pl.ds(i, 1))

    def whole(array):
        return array, array.shape, None

    def over_modes(array):
        return lax.all_to_all(array, "mode", split_axis=0, concat_axis=0, tiled=True)

    def run_spread(layers, *halos):
        sent = f32(blocks, metals, each, len(layers) + 1, part, width)
        (out,) = staged(
            functools.partial(spread_kernel, layers),
            metals,
            [by_metal(field), whole(velocity), whole(dispersion)] + [by_metal(h) for h in halos[:4]],
            [by_unit(sent)],
            20 * math.prod(sent.shape),
            "spread",
            halos[4:],
            arrived=(3, 4, 5, 6) if halos else (),
        )
        return out

    def run_first(layers, got, pieces):
        count = len(layers)
        shapes = [f32(metals, count, part, modes, width), f32(metals, count, 2, modes, width)]
        shapes += [f32(metals, count // pieces, part, modes, width)] * pieces
        return staged(
            functools.partial(first_kernel, layers),
            metals,
            [by_unit(got), by_metal(weights), whole(cls)],
            [by_metal(s) for s in shapes],
            300 * math.prod(got.shape),
            "first",
            arrived=(0,),
        )

    def run_second(layers, g, low, high, l, beside, *halos):
        sent = f32(blocks, metals, each, len(layers), part, width)
        (out,) = staged(
            functools.partial(second_kernel, layers),
            metals,
            [by_metal(a) for a in (g, low, high, l, beside, weights)]
            + [whole(cls), whole(vel), whole(disp)]
            + [by_metal(a) for a in halos[:4]],
            [by_unit(sent)],
            300 * math.prod(sent.shape),
            "second",
            halos[4:],
            arrived=(9, 10, 11, 12) if halos else (),
        )
        return out

    def run_middle(got, g, l, beside):
        sent = f32(blocks, metals, each, len(inner), part, width)
        shapes = [f32(metals, len(outer), part, modes, width), f32(metals, len(outer), 2, modes, width)]
        shapes += [f32(metals, 2, part, modes, width)] * 2

        def body(got, w, cls, g, l, beside, vel, disp, l_outer, beside_outer, low, high, out):
            first_kernel(outer, got, w, cls, l_outer, beside_outer, low, high)
            second_kernel(inner, g, low, high, l, beside, w, cls, vel, disp, out)

        return staged(
            body,
            metals,
            [by_unit(got), by_metal(weights), whole(cls)]
            + [by_metal(a) for a in (g, l, beside)]
            + [whole(vel), whole(disp)],
            [by_metal(s) for s in shapes] + [by_unit(sent)],
            600 * math.prod(got.shape),
            "middle",
            arrived=(0,),
            limit=58 * 1024 * 1024,
        )

    def run_last(pair, got, *so_far):
        block = (1, each, 2, rows, width)

        def at(i):
            return pl.ds(i // 2, 1), slice(None), pl.ds(2 * pair(i % 2), 2)

        (out,) = staged(
            last_kernel,
            2 * metals,
            [
                (field, block, at),
                (
                    got,
                    (blocks, 1, each, 2, part, width),
                    lambda i: (slice(None), pl.ds(i // 2, 1), slice(None), pl.ds(2 * (i % 2), 2)),
                ),
            ],
            [(field, block, at)],
            math.prod(got.shape),
            "last",
            so_far=so_far,
            arrived=(1,),
        )
        return out

    sides = exchange(field[:, :, :2], field[:, :, depth - 2 :], 2)
    got_inner = over_modes(run_spread(inner))
    spread_outer = run_spread(outer, *sides)
    spread_outer, got_inner = after((spread_outer, got_inner))
    got_outer = over_modes(spread_outer)
    l_inner, beside_inner, g = run_first(inner, got_inner, 1)
    g, got_outer = after((g, got_outer))
    l_outer, beside_outer, low, high, back_inner = run_middle(got_outer, g, l_inner, beside_inner)
    sides = exchange(low, high, 1)
    back_inner = over_modes(back_inner)
    back_outer = run_second(outer, g, low, high, l_outer, beside_outer, *sides)
    back_outer, back_inner = after((back_outer, back_inner))
    back_outer = over_modes(back_outer)
    out = run_last(lambda k: k + 1, back_inner)
    return run_last(lambda k: 3 * k, back_outer, out)


def solution(mesh):
    in_specs = (
        P(None, "mode", "space", None, None),
        P("space", None, None),
        P("space", None, None),
        P(),
        P("space", None, None),
        P("space", None, None),
    )
    out_specs = P(None, "mode", "space", None, None)
    return jax.shard_map(
        on_device, mesh=mesh, in_specs=in_specs, out_specs=out_specs, check_vma=False
    )
```

```python
import functools
import math

import jax
import jax.numpy as jnp
import numpy as np
from jax import lax
from jax.experimental import pallas as pl
from jax.experimental.pallas import tpu as pltpu
from jax.sharding import PartitionSpec as P


TIME_STEP = 0.1
MOBILE_BASE = 0.7
RUN = 8
RELAYS = (((6, 1), (1, 6)), ((2, 5), (5, 2)))
SHARED_LIMIT = 50 * 1024 * 1024
VMEM_LIMIT = 61 * 1024 * 1024


def legendre_weight(order):
    return math.comb(2 * order, order) / 4.0**order


def triple_table(terms_count):
    table = np.zeros((terms_count,) * 3, np.float64)
    for a in range(terms_count):
        for b in range(terms_count):
            for c in range(terms_count):
                total = a + b + c
                half = total // 2
                if total % 2 == 0 and max(a, b, c) <= half:
                    amount = legendre_weight(half - a) * legendre_weight(half - b) * legendre_weight(half - c)
                    amount = amount / legendre_weight(half) / (total + 1)
                    table[a, b, c] = amount * math.sqrt((2 * a + 1) * (2 * b + 1) * (2 * c + 1))
    return table.astype(np.float32)


def class_weights(mobility):
    metals, classes, modes = mobility.shape
    triple = jnp.asarray(triple_table(modes))
    mats = jnp.einsum("ijk,mck->mcij", triple, mobility, precision=lax.Precision.HIGHEST)
    mats = TIME_STEP * (mats + MOBILE_BASE * jnp.eye(modes, dtype=jnp.float32))
    mats = mats.reshape(metals, classes * modes, modes)
    high = lax.reduce_precision(mats, exponent_bits=8, mantissa_bits=7)
    return jnp.concatenate([high, high, mats - high], axis=2).astype(jnp.bfloat16)


def lane_neighbours(v):
    lane = lax.broadcasted_iota(jnp.int32, v.shape, v.ndim - 1)
    size = v.shape[-1]
    lower = jnp.where(lane == 0, 0.0, pltpu.roll(v, 1, v.ndim - 1))
    upper = jnp.where(lane == size - 1, 0.0, pltpu.roll(v, size - 1, v.ndim - 1))
    return lower + upper


def combine(l2, l1, mid, r1, r2, sides, vel, disp):
    spread = (16.0 / 12.0) * (l1 + r1) - (1.0 / 12.0) * (l2 + r2) - 6.5 * mid + sides
    carried = (1.0 / 3.0) * r1 + 0.5 * mid - l1 + (1.0 / 6.0) * l2
    return disp * spread - vel * carried


def spread_kernel(layers, f_ref, vel_ref, disp_ref, *rest):
    lo_ref, hi_ref, *around_refs, ends_ref = rest[:5] if len(rest) == 6 else (None,) * 5
    out_ref = rest[-1]
    depth, rows, width = f_ref.shape[2:]
    blocks = out_ref.shape[0]
    part = rows // blocks
    count = len(layers)
    row = lax.broadcasted_iota(jnp.int32, (rows, width), 0)

    def layer(e, x):
        if x < 0:
            return lo_ref[0, e, x + 2] + ends_ref[0] * around_refs[x + 2][0, e, 0]
        if x >= depth:
            return hi_ref[0, e, x - depth] + ends_ref[1] * around_refs[x - depth][0, e, 0]
        return f_ref[0, e, x]

    zero_row = jnp.zeros((1, width), jnp.float32)
    for e in range(f_ref.shape[1]):
        for i, x in enumerate(layers):
            mid = layer(e, x)
            sides = lane_neighbours(mid)
            sides += jnp.where(row == 0, 0.0, pltpu.roll(mid, 1, 0))
            sides += jnp.where(row == rows - 1, 0.0, pltpu.roll(mid, rows - 1, 0))
            around = [layer(e, x + k) for k in (-2, -1, 0, 1, 2)]
            value = combine(*around, sides, vel_ref[x], disp_ref[x])
            for b in range(blocks):
                out_ref[b, 0, e, i] = value[b * part : (b + 1) * part]
                below = value[b * part - 1 : b * part] if b else zero_row
                above = value[(b + 1) * part : (b + 1) * part + 1] if b < blocks - 1 else zero_row
                out_ref[b, 0, e, count, i : i + 1] = below
                out_ref[b, 0, e, count, count + i : count + i + 1] = above


def couple(value, weights, classes, cls_row):
    modes, width = value.shape
    high = value.astype(jnp.bfloat16)
    low = (value - high.astype(jnp.float32)).astype(jnp.bfloat16)
    stacked = jnp.concatenate([high, low, high], axis=0)
    mixed = jnp.dot(weights, stacked, preferred_element_type=jnp.float32)
    picked = jnp.broadcast_to(cls_row, (8, width))
    totals = [jnp.zeros((8, width), jnp.float32)] * (modes // 8)
    for c in range(classes):
        here = picked == c
        for k in range(modes // 8):
            at = c * modes + 8 * k
            totals[k] = jnp.where(here, mixed[at : at + 8], totals[k])
    return jnp.concatenate(totals, axis=0)


def first_kernel(layers, r_ref, w_ref, cls_ref, l_ref, beside_ref, *g_refs):
    sources, _, each, slots, part, width = r_ref.shape
    modes = sources * each
    count = len(layers)
    share = count // len(g_refs)
    classes = w_ref.shape[1] // modes
    weights = w_ref[0]
    for s in range(slots):
        values = jnp.swapaxes(r_ref[:, 0, :, s].reshape(modes, part, width), 0, 1)
        for y in range(part):
            if s < count:
                x, row = layers[s], y + 1
            else:
                x, row = layers[y % count], (part + 1) * (y // count)
            got = couple(values[y], weights, classes, cls_ref[x, row : row + 1])
            if s < count:
                l_ref[0, s, y] = values[y]
                g_refs[s // share][0, s % share, y] = got
            else:
                beside_ref[0, y % count, y // count] = got


def second_kernel(layers, g_ref, low_ref, high_ref, l_ref, beside_ref, w_ref, cls_ref, vel_ref, disp_ref, *rest):
    lo_ref, hi_ref, *around_refs, ends_ref = rest[:5] if len(rest) == 6 else (None,) * 5
    out_ref = rest[-1]
    inner, part, modes, width = g_ref.shape[1:]
    depth = inner + 4
    targets, _, each = out_ref.shape[:3]
    classes = w_ref.shape[1] // modes
    weights = w_ref[0]

    def at(x, y):
        if x < 0:
            return lo_ref[0, x + 2, y] + ends_ref[0] * around_refs[x + 2][0, 0, y]
        if x < 2:
            return low_ref[0, x, y]
        if x < depth - 2:
            return g_ref[0, x - 2, y]
        if x < depth:
            return high_ref[0, x - depth + 2, y]
        return hi_ref[0, x - depth, y] + ends_ref[1] * around_refs[x - depth][0, 0, y]

    for i, x in enumerate(layers):
        rows = []
        for y in range(part):
            mid = at(x, y)
            below = at(x, y - 1) if y else beside_ref[0, i, 0]
            above = at(x, y + 1) if y < part - 1 else beside_ref[0, i, 1]
            sides = lane_neighbours(mid) + (below + above)
            vel = jnp.broadcast_to(vel_ref[x, y : y + 1], (modes, width))
            disp = jnp.broadcast_to(disp_ref[x, y : y + 1], (modes, width))
            value = combine(at(x - 2, y), at(x - 1, y), mid, at(x + 1, y), at(x + 2, y), sides, vel, disp)
            value += 2.0 * l_ref[0, i, y]
            rows.append(couple(value, weights, classes, cls_ref[x, y + 1 : y + 2]))
        out_ref[:, 0, :, i] = jnp.swapaxes(jnp.stack(rows), 0, 1).reshape(targets, each, part, width)


def last_kernel(f_ref, r_ref, *rest):
    out_ref = rest[-1]
    blocks = r_ref.shape[0]
    part = r_ref.shape[4]
    for b in range(blocks):
        rows = slice(b * part, (b + 1) * part)
        out_ref[0, :, :, rows] = f_ref[0, :, :, rows] + r_ref[b, 0]


def staged(body, steps, inputs, outputs, flops, name, scalars=(), so_far=(), arrived=(), limit=SHARED_LIMIT):
    n_in, n_out = len(inputs), len(outputs)

    def kernel(*refs):
        in_refs, refs = refs[:n_in], refs[n_in:]
        scalar_refs, refs = refs[: len(scalars)], refs[len(scalars) :]
        refs = refs[len(so_far) :]
        out_refs, refs = refs[:n_out], refs[n_out:]
        in_bufs, out_bufs, (sems,) = refs[:n_in], refs[n_in : n_in + n_out], refs[n_in + n_out :]

        def load(k, i):
            index = inputs[k][2]
            if index is None:
                return pltpu.make_async_copy(in_refs[k], in_bufs[k], sems.at[k, 0])
            return pltpu.make_async_copy(in_refs[k].at[index(i)], in_bufs[k].at[i], sems.at[k, i])

        def store(k, i):
            return pltpu.make_async_copy(out_bufs[k].at[i], out_refs[k].at[outputs[k][2](i)], sems.at[n_in + k, i])

        for i in range(steps):
            for k in range(n_in):
                if i == 0 or inputs[k][2] is not None:
                    load(k, i).start()
        for k in range(n_in):
            if inputs[k][2] is None:
                load(k, 0).wait()

        def step(i, carry):
            for k in range(n_in):
                if inputs[k][2] is not None:
                    load(k, i).wait()
            blocks = [buf if spec[2] is None else buf.at[i] for buf, spec in zip(in_bufs, inputs)]
            body(*blocks, *scalar_refs, *[buf.at[i] for buf in out_bufs])
            for k in range(n_out):
                store(k, i).start()
            return carry

        lax.fori_loop(0, steps, step, 0)
        for i in range(steps):
            for k in range(n_out):
                store(k, i).wait()

    hbm = pl.BlockSpec(memory_space=pltpu.HBM)
    scratch = [
        pltpu.VMEM(block if index is None else (steps,) + block, array.dtype) for array, block, index in inputs
    ]
    scratch += [pltpu.VMEM((steps,) + block, shape.dtype) for shape, block, _ in outputs]
    moved = sum(4 * math.prod(a.shape) for a, *_ in (*inputs, *outputs))
    return pl.pallas_call(
        kernel,
        in_specs=[pl.BlockSpec(memory_space=pl.ANY) if k in arrived else hbm for k in range(n_in)]
        + [pl.BlockSpec(memory_space=pltpu.SMEM)] * len(scalars) + [hbm] * len(so_far),
        out_specs=[hbm] * n_out,
        out_shape=[pltpu.HBM(shape.shape, shape.dtype) for shape, *_ in outputs],
        scratch_shapes=scratch + [pltpu.SemaphoreType.DMA((n_in + n_out, steps))],
        input_output_aliases={n_in + len(scalars): 0} if so_far else {},
        compiler_params=pltpu.CompilerParams(vmem_limit_bytes=limit if arrived else VMEM_LIMIT),
        cost_estimate=pl.CostEstimate(flops=flops, bytes_accessed=moved, transcendentals=0),
        name=name,
    )(*[array for array, *_ in inputs], *scalars, *so_far)


def halo_routes(space, blocks):
    direct, relayed = [], [([], []), ([], [])]
    for s in range(space - 1):
        for m in range(blocks):
            ends = (s * blocks + m, (s + 1) * blocks + m)
            if (s + 1) % RUN:
                direct.append(ends)
                continue
            for (leave, arrive), relays in zip(relayed, RELAYS):
                up, down = relays[2 * m // blocks]
                near = (s + 1 - RUN + up) * blocks + m
                far = (s + 1 + down) * blocks + m
                leave += [(ends[0], near), (ends[1], far)]
                arrive += [(near, ends[1]), (far, ends[0])]
    return direct, relayed


def on_device(field, velocity, dispersion, mobility, material, fixed_mask):
    metals, each, depth, rows, width = field.shape
    modes = mobility.shape[2]
    classes = mobility.shape[1]
    blocks = lax.axis_size("mode")
    part = rows // blocks
    space = lax.axis_size("space")
    direct, relayed = halo_routes(space, blocks)
    back = [(b, a) for a, b in direct]
    both = ("space", "mode")
    place = lax.axis_index("space") % RUN
    ends = jnp.stack([place == 0, place == RUN - 1]).astype(jnp.float32)

    def exchange(low, high, axis):
        lo = lax.ppermute(high, both, direct)
        hi = lax.ppermute(low, both, back)
        out = jnp.where(place == RUN - 1, high, low)
        around = []
        for layer, (leave, arrive) in enumerate(relayed):
            piece = lax.slice_in_dim(out, layer, layer + 1, axis=axis)
            around.append(lax.ppermute(lax.ppermute(piece, both, leave), both, arrive))
        return lo, hi, *around, ends

    inner = tuple(range(2, depth - 2))
    outer = (0, 1, depth - 2, depth - 1)
    after = lax.optimization_barrier

    weights = class_weights(mobility)
    here = lax.axis_index("mode") * part
    cls = jnp.where(fixed_mask == 1, classes, material)
    cls = lax.dynamic_slice_in_dim(jnp.pad(cls, ((0, 0), (1, 1), (0, 0))), here, part + 2, 1)
    vel = lax.dynamic_slice_in_dim(velocity, here, part, 1)
    disp = lax.dynamic_slice_in_dim(dispersion, here, part, 1)

    def f32(*shape):
        return jax.ShapeDtypeStruct(shape, jnp.float32)

    def by_metal(array):
        return array, (1,) + array.shape[1:], lambda i: pl.ds(i, 1)

    def by_unit(array):
        return array, (array.shape[0], 1) + array.shape[2:], lambda i: (slice(None), pl.ds(i, 1))

    def whole(array):
        return array, array.shape, None

    def over_modes(array):
        return lax.all_to_all(array, "mode", split_axis=0, concat_axis=0, tiled=True)

    def run_spread(layers, *halos):
        sent = f32(blocks, metals, each, len(layers) + 1, part, width)
        (out,) = staged(
            functools.partial(spread_kernel, layers),
            metals,
            [by_metal(field), whole(velocity), whole(dispersion)] + [by_metal(h) for h in halos[:4]],
            [by_unit(sent)],
            20 * math.prod(sent.shape),
            "spread",
            halos[4:],
            arrived=(3, 4, 5, 6) if halos else (),
        )
        return out

    def run_first(layers, got, pieces):
        count = len(layers)
        shapes = [f32(metals, count, part, modes, width), f32(metals, count, 2, modes, width)]
        shapes += [f32(metals, count // pieces, part, modes, width)] * pieces
        return staged(
            functools.partial(first_kernel, layers),
            metals,
            [by_unit(got), by_metal(weights), whole(cls)],
            [by_metal(s) for s in shapes],
            300 * math.prod(got.shape),
            "first",
            arrived=(0,),
        )

    def run_second(layers, g, low, high, l, beside, *halos):
        sent = f32(blocks, metals, each, len(layers), part, width)
        (out,) = staged(
            functools.partial(second_kernel, layers),
            metals,
            [by_metal(a) for a in (g, low, high, l, beside, weights)]
            + [whole(cls), whole(vel), whole(disp)]
            + [by_metal(a) for a in halos[:4]],
            [by_unit(sent)],
            300 * math.prod(sent.shape),
            "second",
            halos[4:],
            arrived=(9, 10, 11, 12) if halos else (),
        )
        return out

    def run_middle(got, g, l, beside):
        sent = f32(blocks, metals, each, len(inner), part, width)
        shapes = [f32(metals, len(outer), part, modes, width), f32(metals, len(outer), 2, modes, width)]
        shapes += [f32(metals, 2, part, modes, width)] * 2

        def body(got, w, cls, g, l, beside, vel, disp, l_outer, beside_outer, low, high, out):
            first_kernel(outer, got, w, cls, l_outer, beside_outer, low, high)
            second_kernel(inner, g, low, high, l, beside, w, cls, vel, disp, out)

        return staged(
            body,
            metals,
            [by_unit(got), by_metal(weights), whole(cls)]
            + [by_metal(a) for a in (g, l, beside)]
            + [whole(vel), whole(disp)],
            [by_metal(s) for s in shapes] + [by_unit(sent)],
            600 * math.prod(got.shape),
            "middle",
            arrived=(0,),
            limit=58 * 1024 * 1024,
        )

    def run_last(pair, got, *so_far):
        block = (1, each, 2, rows, width)

        def at(i):
            return pl.ds(i // 2, 1), slice(None), pl.ds(2 * pair(i % 2), 2)

        (out,) = staged(
            last_kernel,
            2 * metals,
            [
                (field, block, at),
                (
                    got,
                    (blocks, 1, each, 2, part, width),
                    lambda i: (slice(None), pl.ds(i // 2, 1), slice(None), pl.ds(2 * (i % 2), 2)),
                ),
            ],
            [(field, block, at)],
            math.prod(got.shape),
            "last",
            so_far=so_far,
            arrived=(1,),
        )
        return out

    sides = exchange(field[:, :, :2], field[:, :, depth - 2 :], 2)
    got_inner = over_modes(run_spread(inner))
    spread_outer = run_spread(outer, *sides)
    spread_outer, got_inner = after((spread_outer, got_inner))
    got_outer = over_modes(spread_outer)
    l_inner, beside_inner, g = run_first(inner, got_inner, 1)
    g, got_outer = after((g, got_outer))
    l_outer, beside_outer, low, high, back_inner = run_middle(got_outer, g, l_inner, beside_inner)
    sides = exchange(low, high, 1)
    back_inner = over_modes(back_inner)
    back_outer = run_second(outer, g, low, high, l_outer, beside_outer, *sides)
    back_outer, back_inner = after((back_outer, back_inner))
    back_outer = over_modes(back_outer)
    out = run_last(lambda k: k + 1, back_inner)
    return run_last(lambda k: 3 * k, back_outer, out)


def solution(mesh):
    in_specs = (
        P(None, "mode", "space", None, None),
        P("space", None, None),
        P("space", None, None),
        P(),
        P("space", None, None),
        P("space", None, None),
    )
    out_specs = P(None, "mode", "space", None, None)
    return jax.shard_map(
        on_device, mesh=mesh, in_specs=in_specs, out_specs=out_specs, check_vma=False
    )
```
